32 devices in a mesh: parts: 2 (over x), chan: 16 (over z, y, core).
Axes of the slice: x: 2, y: 2, z: 4, core: 2. Of those that a mesh axis runs over, the one named last changes fastest.
Arguments:
- recording: float32 [4096, 599], P(('parts', 'chan')), parts along dimension 0, may hold values from -120 to 120
- alive: int32 [4096], P(('parts', 'chan')), parts along dimension 0, may hold values from 0 to 1
- bank: bfloat16 [512, 400, 200], P(('parts', 'chan')), parts along dimension 0, may hold values from -150 to 150
- start: int32 [512], P(('parts', 'chan')), parts along dimension 0, may hold values from 0 to 2047, as said below
Outputs:
- scores: float32 [512, 400], P(('parts', 'chan')), parts along dimension 0
- peaks: float32 [800], P('parts'), parts along dimension 0
The draws below stay inside these ranges and needn't reach their ends.
There are 2 independent parts, one for each index of `parts`. The reference program is written for one: setup_inputs(seed, part) draws one part's arguments, and reference() takes and returns one part's arrays. A program takes and returns all parts, laid end to end along the dimension named above; each array names one. Nothing has to cross between parts.
Inputs may be any that keep to these rules, and one draw needn't show every extreme that they name: `start`: template k starts in channel group k // 16: from 128 * (k // 16) to 128 * (k // 16) + 127; in every group some template starts at the group's last channel.
All inputs are finite; a program needn't handle non-finite values.
Results may differ from the reference program's by a relative error of at most 0.00046.
Values sent between devices are 32-bit elements; how exact they have to be, the bound alone decides.
A program may use at most 64 MiB of HBM per device.

```python
import math
import jax
import jax.numpy as jnp
from jax import lax

TCH = 400
TS = 200
CH_DEV = 128
TMP_DEV = 16
LAGS = 400
LEN = 599
CHANNELS = 2048
TEMPLATES = 256


def channel_field(key):
    envelope = jnp.exp(jax.random.uniform(jax.random.fold_in(key, 102), (LEN,), jnp.float32, math.log(0.3), math.log(3.0)))
    channel_gain = jnp.exp(jax.random.uniform(jax.random.fold_in(key, 101), (CHANNELS,), jnp.float32, math.log(0.3), math.log(3.0)))
    noise_part = jnp.clip(jax.random.normal(jax.random.fold_in(key, 103), (CHANNELS, LEN), jnp.float32), -5.0, 5.0)
    field_data = channel_gain[:, None] * envelope[None, :] * noise_part
    return (field_data, channel_gain)


def dead_mask(key):
    return (jax.random.randint(jax.random.fold_in(key, 401), (CHANNELS,), 0, 8) != 0).astype(jnp.int32)


def template_starts(key):
    groups = CHANNELS // CH_DEV
    offsets = jax.random.randint(jax.random.fold_in(key, 501), (groups, TMP_DEV), 0, CH_DEV)
    chosen = jax.random.randint(jax.random.fold_in(key, 502), (groups,), 0, TMP_DEV)
    offsets = jnp.where(jnp.arange(TMP_DEV)[None, :] == chosen[:, None], CH_DEV - 1, offsets)
    starts = offsets + CH_DEV * jnp.arange(groups)[:, None]
    return starts.reshape(-1).astype(jnp.int32)


def draw_recording(key, part):
    field_data, channel_gain = channel_field(key)
    living = dead_mask(key)
    garbage = 5.0 * channel_gain[:, None] * jnp.clip(jax.random.normal(jax.random.fold_in(key, 301), (CHANNELS, LEN), jnp.float32), -5.0, 5.0)
    return jnp.where(living[:, None] == 1, field_data, garbage)


def draw_alive(key, part):
    return dead_mask(key)


def draw_start(key, part):
    return template_starts(key)


def draw_bank(key, part):
    field_data, channel_gain = channel_field(key)
    padded = jnp.pad(field_data, ((0, TCH), (0, 0)))
    gain_pad = jnp.pad(channel_gain, (0, TCH), constant_values=1.0)
    first_rows = template_starts(key)
    lag_pick = jax.random.randint(jax.random.fold_in(key, 201), (TEMPLATES,), 0, LAGS)
    spread_level = jnp.exp(jax.random.uniform(jax.random.fold_in(key, 202), (TEMPLATES,), jnp.float32, math.log(0.3), math.log(3.0)))
    noise_key = jax.random.fold_in(key, 203)

    def one_template(slot_id):
        window = lax.dynamic_slice(padded, (first_rows[slot_id], lag_pick[slot_id]), (TCH, TS))
        scale_rows = lax.dynamic_slice_in_dim(gain_pad, first_rows[slot_id], TCH)
        noise_part = jnp.clip(jax.random.normal(jax.random.fold_in(noise_key, slot_id), (TCH, TS), jnp.float32), -5.0, 5.0)
        return (window + spread_level[slot_id] * scale_rows[:, None] * noise_part).astype(jnp.bfloat16)
    return lax.map(one_template, jnp.arange(TEMPLATES))


def setup_inputs(seed: int = 0, part: int = 0) -> dict:
    keys = jax.random.split(jax.random.key(seed), 5)
    own_keys = jax.random.split(jax.random.fold_in(keys[4], part), 5)
    recording = draw_recording(jax.random.fold_in(jax.random.fold_in(keys[4], part), 71), part)
    alive = draw_alive(jax.random.fold_in(jax.random.fold_in(keys[4], part), 71), part)
    bank = draw_bank(jax.random.fold_in(jax.random.fold_in(keys[4], part), 71), part)
    start = draw_start(jax.random.fold_in(jax.random.fold_in(keys[4], part), 71), part)
    return {"recording": recording, "alive": alive, "bank": bank, "start": start}


epsilon = 1e-06

def reference(recording, alive, bank, start):
    channels, length = recording.shape
    templates, tmpl_chans, tmpl_len = bank.shape
    lag_count = length - tmpl_len + 1
    living = alive.astype(jnp.float32)
    masked = recording * living[:, None]
    rounded = lax.optimization_barrier(masked.astype(jnp.bfloat16)).astype(jnp.float32)
    fft_size = 1 << (length - 1).bit_length()
    spectrum = jnp.fft.rfft(jnp.pad(rounded, ((0, tmpl_chans), (0, 0))), n=fft_size, axis=1)
    sample_ids = jnp.arange(length)[:, None]
    lag_ids = jnp.arange(lag_count)[None, :]
    box_sum = ((sample_ids >= lag_ids) & (sample_ids < lag_ids + tmpl_len)).astype(jnp.float32)
    energy = jnp.dot(jnp.square(masked), box_sum, precision=lax.Precision.HIGHEST)
    energy = jnp.pad(energy, ((0, tmpl_chans), (0, 0)))
    live_pad = jnp.pad(living, (0, tmpl_chans))
    block_size = 64

    def one_block(block_item):
        tmpl_tiles, first_rows = block_item
        tiles_wide = tmpl_tiles.astype(jnp.float32)
        tile_spec = jnp.fft.rfft(tiles_wide, n=fft_size, axis=2)

        def spec_rows(row_start):
            return lax.dynamic_slice_in_dim(spectrum, row_start.astype(jnp.int32), tmpl_chans, 0)

        def energy_rows(row_start):
            return lax.optimization_barrier(jnp.sum(lax.dynamic_slice_in_dim(energy, row_start.astype(jnp.int32), tmpl_chans, 0), axis=0))

        def live_rows(row_start):
            return lax.dynamic_slice_in_dim(live_pad, row_start.astype(jnp.int32), tmpl_chans, 0)
        data_spec = jax.vmap(spec_rows)(first_rows)
        summed = lax.optimization_barrier(jnp.sum(data_spec * jnp.conj(tile_spec), axis=1))
        crossed = jnp.fft.irfft(summed, n=fft_size, axis=1)[:, :lag_count]
        data_energy = jax.vmap(energy_rows)(first_rows)
        tmpl_energy = lax.optimization_barrier(jnp.sum(jax.vmap(live_rows)(first_rows) * lax.optimization_barrier(jnp.sum(jnp.square(tiles_wide), axis=2)), axis=1))
        return crossed * lax.rsqrt(tmpl_energy[:, None] * data_energy + epsilon)
    grouped = (bank.reshape(templates // block_size, block_size, tmpl_chans, tmpl_len), start.reshape(templates // block_size, block_size))
    scores = lax.map(one_block, grouped).reshape(templates, lag_count)
    return (scores, lax.optimization_barrier(jnp.max(scores, axis=0)))
```

```python
import functools

import jax
import jax.numpy as jnp
from jax import lax
from jax.experimental import pallas as pl
from jax.experimental.pallas import tpu as pltpu
from jax.sharding import PartitionSpec as P

epsilon = 1e-06
LANES = 128
SUB = 8
MESH = pl.DeviceIdType.MESH


def up(value, unit):
    return -(-value // unit) * unit


def left(x, by):
    by = by % x.shape[-1]
    return x if by == 0 else pltpu.roll(x, x.shape[-1] - by, x.ndim - 1)


def kernel(
    size, tmpl_chans, tmpl_len, length, lag_count,
    start_ref, alive_ref, rec_hbm, bank_hbm,
    scores_ref, peaks_ref,
    rec_v, bank_v, bank_t, tsq, xw, live, esum, qsum, tsum, pk,
    rec_sem, bank_sem, send_sem, recv_sem, pk_send, pk_recv,
):
    me = lax.axis_index("chan")
    ch_dev = rec_v.shape[0]
    tmp_dev = bank_v.shape[0]
    panels, rows, _ = xw.shape
    wide = panels * LANES
    lag_wide = up(lag_count + SUB - 1, LANES)
    reach = -(-rows // ch_dev) - 1
    tail_lane = length - (panels - 1) * LANES

    barrier = pltpu.get_barrier_semaphore()

    def greet(d, _):
        pl.semaphore_signal(
            barrier, inc=1, device_id={"chan": lax.rem(me + d, size)}, device_id_type=MESH
        )
        return 0

    lax.fori_loop(1, size, greet, 0)

    rec_copy = pltpu.make_async_copy(rec_hbm, rec_v, rec_sem)
    rec_copy.start()
    bank_copies = [
        pltpu.make_async_copy(bank_hbm.at[k], bank_v.at[k], bank_sem.at[k])
        for k in range(tmp_dev)
    ]
    for copy in bank_copies:
        copy.start()

    diagonal = lax.broadcasted_iota(jnp.int32, (ch_dev, ch_dev), 0) == lax.broadcasted_iota(
        jnp.int32, (ch_dev, ch_dev), 1
    )
    flags = jnp.sum(
        jnp.where(diagonal, alive_ref[...].astype(jnp.float32), 0.0), axis=1, keepdims=True
    )
    rec_copy.wait()
    for p in range(panels - 1):
        xw[p, :ch_dev, :] = rec_v[:, p * LANES : (p + 1) * LANES] * flags
    lane = lax.broadcasted_iota(jnp.int32, (ch_dev, LANES), 1)
    xw[panels - 1, :ch_dev, :] = jnp.where(lane == tail_lane, flags, 0.0)
    xw[panels - 1, :ch_dev, :tail_lane] = rec_v[:, (panels - 1) * LANES : length] * flags

    pl.semaphore_wait(barrier, size - 1)

    sends = []
    for d in range(1, reach + 1):
        count = min(ch_dev, rows - d * ch_dev)
        copy = pltpu.make_async_remote_copy(
            src_ref=xw.at[:, pl.ds(0, count), :],
            dst_ref=xw.at[:, pl.ds(d * ch_dev, count), :],
            send_sem=send_sem.at[d - 1],
            recv_sem=recv_sem.at[d - 1],
            device_id={"chan": lax.rem(me - d + size, size)},
            device_id_type=MESH,
        )
        sends.append(copy)

        @pl.when(me >= d)
        def _(copy=copy):
            copy.start()

        @pl.when(me + d >= size)
        def _(d=d, count=count):
            xw[:, d * ch_dev : d * ch_dev + count, :] = jnp.zeros(
                (panels, count, LANES), jnp.float32
            )

    rest = tmpl_len - LANES
    rest_lane = lax.broadcasted_iota(jnp.int32, (tmpl_chans, LANES), 1)

    def prepare(k, _):
        pltpu.make_async_copy(bank_hbm.at[k], bank_v.at[k], bank_sem.at[k]).wait()
        tile = bank_v[k]
        bank_t[k] = tile.T
        first = tile[:, :LANES].astype(jnp.float32)
        second = tile[:, LANES:].astype(jnp.float32)
        second = jnp.concatenate(
            [second, jnp.zeros((tmpl_chans, LANES - rest), jnp.float32)], axis=1
        )
        tsq[k] = first * first + second * second
        return 0

    lax.fori_loop(0, tmp_dev, prepare, 0)

    for d in range(1, reach + 1):

        @pl.when(me + d < size)
        def _(copy=sends[d - 1]):
            copy.wait_recv()

    live[...] = jnp.broadcast_to(xw[panels - 1, :, tail_lane : tail_lane + 1], live.shape)

    def fold(x):
        return jnp.sum(x.reshape(x.shape[0] // SUB, SUB, x.shape[1]), axis=0)

    def correlate(k, _):
        first = jnp.clip(start_ref[k] - me * ch_dev, 0, ch_dev - 1)
        parts = [xw[p, pl.ds(first, tmpl_chans), :] for p in range(panels)]
        row = pl.ds(pl.multiple_of(k * SUB, SUB), SUB)
        for p in range(panels):
            qsum[p, row, :] = fold(parts[p] * parts[p])
        tsum[row, :] = fold(live[pl.ds(first, tmpl_chans), :] * tsq[k])
        data = jnp.concatenate([part.astype(jnp.bfloat16) for part in parts], axis=1)
        acc = jnp.dot(bank_t[k], data, preferred_element_type=jnp.float32)
        half = LANES
        high = acc[half:]
        short = high.shape[0]
        low = jnp.concatenate(
            [acc[:short, : wide - half] + high[:, half:], acc[short:half, : wide - half]], axis=0
        )
        acc = jnp.concatenate([low, acc[:half, wide - half :]], axis=1)
        half //= 2
        acc = (acc[:half] + left(acc[half:], half))[:, :lag_wide]
        while half > SUB:
            half //= 2
            acc = acc[:half] + left(acc[half:], half)
        for p in range(lag_wide // LANES):
            esum[p, row, :] = acc[:, p * LANES : (p + 1) * LANES]
        return 0

    lax.fori_loop(0, tmp_dev, correlate, 0)

    crossed = jnp.zeros((tmp_dev, lag_wide), jnp.float32)
    energy = jnp.zeros((tmp_dev, wide), jnp.float32)
    tmpl_energy = jnp.zeros((tmp_dev, LANES), jnp.float32)
    for b in range(SUB):
        pick = pl.ds(b, tmp_dev, stride=SUB)
        crossed = crossed + left(
            jnp.concatenate([esum[p, pick, :] for p in range(lag_wide // LANES)], axis=1), b
        )
        energy = energy + jnp.concatenate([qsum[p, pick, :] for p in range(panels)], axis=1)
        tmpl_energy = tmpl_energy + tsum[pick, :]
    tmpl_energy = jnp.sum(tmpl_energy, axis=1, keepdims=True)
    box = None
    done = 0
    span = 1
    for bit in range(tmpl_len.bit_length()):
        if tmpl_len & span:
            moved = left(energy, done)
            box = moved if box is None else box + moved
            done += span
        if 2 * span <= tmpl_len:
            energy = energy + left(energy, span)
        span *= 2
    scores = crossed * lax.rsqrt(tmpl_energy * box[:, :lag_wide] + epsilon)
    scores_ref[...] = scores[:, :lag_count]

    pk[me] = jnp.max(scores, axis=0, keepdims=True)

    def swap(d):
        other = lax.rem(me + d, size)
        return pltpu.make_async_remote_copy(
            src_ref=pk.at[me],
            dst_ref=pk.at[me],
            send_sem=pk_send.at[d],
            recv_sem=pk_recv.at[d],
            device_id={"chan": other},
            device_id_type=MESH,
        )

    def swap_start(d, _):
        swap(d).start()
        return 0

    def swap_done(d, _):
        swap(d).wait_recv()
        return 0

    def swap_sent(d, _):
        swap(d).wait_send()
        return 0

    lax.fori_loop(1, size, swap_start, 0)
    lax.fori_loop(1, size, swap_done, 0)
    peaks_ref[...] = jnp.max(pk[...], axis=0)[:, :lag_count]
    lax.fori_loop(1, size, swap_sent, 0)
    for d in range(1, reach + 1):

        @pl.when(me >= d)
        def _(copy=sends[d - 1]):
            copy.wait_send()


def local(recording, alive, bank, start):
    ch_dev, length = recording.shape
    tmp_dev, tmpl_chans, tmpl_len = bank.shape
    lag_count = length - tmpl_len + 1
    size = lax.axis_size("chan")
    panels = -(-(length + 1) // LANES)
    rows = up(ch_dev + tmpl_chans - 1, SUB * 2)
    reach = -(-rows // ch_dev) - 1
    lag_wide = up(lag_count + SUB - 1, LANES)
    vmem = pl.BlockSpec(memory_space=pltpu.VMEM)
    anywhere = pl.BlockSpec(memory_space=pl.ANY)
    scores, peaks = pl.pallas_call(
        functools.partial(kernel, size, tmpl_chans, tmpl_len, length, lag_count),
        out_shape=(
            jax.ShapeDtypeStruct((tmp_dev, lag_count), jnp.float32),
            jax.ShapeDtypeStruct((1, lag_count), jnp.float32),
        ),
        in_specs=[pl.BlockSpec(memory_space=pltpu.SMEM), vmem, anywhere, anywhere],
        out_specs=(vmem, vmem),
        scratch_shapes=[
            pltpu.VMEM((ch_dev, length), jnp.float32),
            pltpu.VMEM((tmp_dev, tmpl_chans, tmpl_len), bank.dtype),
            pltpu.VMEM((tmp_dev, tmpl_len, tmpl_chans), bank.dtype),
            pltpu.VMEM((tmp_dev, tmpl_chans, LANES), jnp.float32),
            pltpu.VMEM((panels, rows, LANES), jnp.float32),
            pltpu.VMEM((rows, LANES), jnp.float32),
            pltpu.VMEM((lag_wide // LANES, tmp_dev * SUB, LANES), jnp.float32),
            pltpu.VMEM((panels, tmp_dev * SUB, LANES), jnp.float32),
            pltpu.VMEM((tmp_dev * SUB, LANES), jnp.float32),
            pltpu.VMEM((size, 1, lag_wide), jnp.float32),
            pltpu.SemaphoreType.DMA(()),
            pltpu.SemaphoreType.DMA((tmp_dev,)),
            pltpu.SemaphoreType.DMA((reach,)),
            pltpu.SemaphoreType.DMA((reach,)),
            pltpu.SemaphoreType.DMA((size,)),
            pltpu.SemaphoreType.DMA((size,)),
        ],
        compiler_params=pltpu.CompilerParams(
            collective_id=0, has_side_effects=True, vmem_limit_bytes=48 * 1024 * 1024
        ),
    )(start, alive.reshape(1, ch_dev), recording, bank)
    return scores, peaks.reshape(lag_count)


def solution(mesh):
    placed = (
        P(("parts", "chan"), None),
        P(("parts", "chan")),
        P(("parts", "chan"), None, None),
        P(("parts", "chan")),
    )
    return jax.shard_map(
        local,
        mesh=mesh,
        in_specs=placed,
        out_specs=(P(("parts", "chan"), None), P("parts")),
        check_vma=False,
    )
```

```python
import functools

import jax
import jax.numpy as jnp
from jax import lax
from jax.experimental import pallas as pl
from jax.experimental.pallas import tpu as pltpu
from jax.sharding import PartitionSpec as P

epsilon = 1e-06
LANES = 128
SUB = 8
HALVES = 2
MESH = pl.DeviceIdType.MESH


def up(value, unit):
    return -(-value // unit) * unit


def left(x, by):
    by = by % x.shape[-1]
    return x if by == 0 else pltpu.roll(x, x.shape[-1] - by, x.ndim - 1)


def kernel(
    size, tmpl_chans, tmpl_len, length, lag_count,
    start_ref, alive_ref, rec_hbm, bank_hbm,
    scores_ref, peaks_ref,
    rec_v, turn, bank_v, bank_t, tsq, xw, relay, live, esum, qsum, tsum, pk,
    rec_sem, bank_sem, send_sem, recv_sem, relay_sem, pk_send, pk_recv,
):
    me = lax.axis_index("chan")
    ch_dev = rec_v.shape[1]
    tmp_dev = bank_v.shape[0]
    panels, rows, _ = xw.shape
    wide = panels * LANES
    lag_wide = up(lag_count + SUB - 1, LANES)
    reach = -(-rows // ch_dev) - 1
    tail_lane = length - (panels - 1) * LANES

    barrier = pltpu.get_barrier_semaphore()

    def greet(d, _):
        pl.semaphore_signal(
            barrier, inc=1, device_id={"chan": lax.rem(me + d, size)}, device_id_type=MESH
        )
        return 0

    lax.fori_loop(1, size, greet, 0)

    rec_copy = pltpu.make_async_copy(rec_hbm, rec_v, rec_sem)
    rec_copy.start()
    bank_copies = [
        pltpu.make_async_copy(bank_hbm.at[k], bank_v.at[k], bank_sem.at[k])
        for k in range(tmp_dev)
    ]
    for copy in bank_copies:
        copy.start()

    flags = alive_ref[...].astype(jnp.float32)
    turn[...] = jnp.zeros(turn.shape, jnp.float32)
    turn[tail_lane : tail_lane + 1, :] = flags
    rec_copy.wait()
    for p in range(panels - 1):
        xw[p, :ch_dev, :] = (rec_v[p * LANES : (p + 1) * LANES, :] * flags).T
    turn[:tail_lane, :] = rec_v[(panels - 1) * LANES : length, :] * flags
    xw[panels - 1, :ch_dev, :] = turn[...].T

    pl.semaphore_wait(barrier, size - 1)

    part = ch_dev // HALVES
    role = lax.rem(me, 4)
    further = me >= 4
    sent = []

    def rows_of(slot, h):
        return pl.ds(slot * ch_dev + h * part, part)

    def send(when, src, dst, arrival, by):
        copy = pltpu.make_async_remote_copy(
            src_ref=src,
            dst_ref=dst,
            send_sem=send_sem.at[len(sent)],
            recv_sem=arrival,
            device_id={"chan": lax.rem(me + by + size, size)},
            device_id_type=MESH,
        )
        sent.append((when, copy))

        @pl.when(when)
        def _():
            copy.start()

    def to_slot(when, from_slot, h, slot, by):
        send(
            when,
            xw.at[:, rows_of(from_slot, h), :],
            xw.at[:, rows_of(slot, h), :],
            recv_sem.at[slot - 1, h],
            by,
        )

    def arrived(slot, h):
        where = xw.at[:, pl.ds(slot * ch_dev, tail) if slot == reach else rows_of(slot, h), :]
        pltpu.make_async_remote_copy(
            src_ref=where,
            dst_ref=where,
            send_sem=send_sem.at[0],
            recv_sem=recv_sem.at[slot - 1, h],
            device_id={"chan": lax.rem(me + 1, size)},
            device_id_type=MESH,
        ).wait_recv()

    is_a, is_b, is_c, is_d = (role == r for r in range(4))
    tail = rows - reach * ch_dev
    for h in range(HALVES):
        send(
            is_b & further,
            xw.at[:, rows_of(0, h), :],
            relay.at[:, pl.ds(h * part, part), :],
            relay_sem.at[h],
            2,
        )
        to_slot((is_a | is_c) & further, 0, h, 3, -3)
        to_slot(is_c | is_d, 0, h, 2, -2)
        to_slot(is_b | is_d, 0, h, 1, -1)
    send(
        further,
        xw.at[:, pl.ds(0, tail), :],
        xw.at[:, pl.ds(reach * ch_dev, tail), :],
        recv_sem.at[reach - 1, 0],
        -4,
    )
    for d in range(1, reach + 1):
        count = min(ch_dev, rows - d * ch_dev)

        @pl.when(me + d >= size)
        def _(d=d, count=count):
            xw[:, d * ch_dev : d * ch_dev + count, :] = jnp.zeros(
                (panels, count, LANES), jnp.float32
            )

    def pass_on(when, from_slot, h, slot, by):
        @pl.when(when)
        def _():
            arrived(from_slot, h)

        to_slot(when, from_slot, h, slot, by)

    def pass_back(h):
        when = is_d & further

        @pl.when(when)
        def _():
            where = relay.at[:, pl.ds(h * part, part), :]
            pltpu.make_async_remote_copy(
                src_ref=where,
                dst_ref=where,
                send_sem=send_sem.at[0],
                recv_sem=relay_sem.at[h],
                device_id={"chan": lax.rem(me + 1, size)},
                device_id_type=MESH,
            ).wait_recv()

        send(
            when,
            relay.at[:, pl.ds(h * part, part), :],
            xw.at[:, rows_of(2, h), :],
            recv_sem.at[1, h],
            -4,
        )

    b_in, d_in = is_b & (me + 3 < size), is_d & (me + 1 < size)

    def relay_round(number):
        if number == 0:
            pass_on(b_in, 3, 0, 1, 2)
            pass_back(0)
        elif number == 1:
            pass_on(b_in, 3, 1, 1, 2)
            pass_back(1)
            pass_on(is_a, 2, 0, 1, 1)
            pass_on(is_b, 2, 0, 3, -1)
        elif number == 2:
            pass_on(d_in, 1, 0, 2, -1)
            pass_on(d_in, 2, 0, 3, -1)
        else:
            pass_on(is_a, 2, 1, 1, 1)
            pass_on(is_b, 2, 1, 3, -1)
            pass_on(d_in, 1, 1, 2, -1)
            pass_on(d_in, 2, 1, 3, -1)

    rest = tmpl_len - LANES
    rest_lane = lax.broadcasted_iota(jnp.int32, (tmpl_chans, LANES), 1)

    def prepare(k, _):
        pltpu.make_async_copy(bank_hbm.at[k], bank_v.at[k], bank_sem.at[k]).wait()
        tile = bank_v[k]
        bank_t[k] = tile.T
        first = tile[:, :LANES].astype(jnp.float32)
        second = tile[:, LANES:].astype(jnp.float32)
        second = jnp.concatenate(
            [second, jnp.zeros((tmpl_chans, LANES - rest), jnp.float32)], axis=1
        )
        tsq[k] = first * first + second * second
        return 0

    share = 3 * tmp_dev // 16
    begin = 0
    for number in range(4):
        end = begin + share
        lax.fori_loop(begin, end, prepare, 0)
        relay_round(number)
        begin = end
    lax.fori_loop(begin, tmp_dev, prepare, 0)

    for d in range(1, reach + 1):
        for h in range(HALVES if d < reach else 1):
            waited = {1: d_in, 2: is_a | is_b | d_in, 3: b_in}.get(d)
            here = me + d < size
            if waited is not None:
                here = here & jnp.logical_not(waited)

            @pl.when(here)
            def _(d=d, h=h):
                arrived(d, h)

    live[...] = jnp.broadcast_to(xw[panels - 1, :, tail_lane : tail_lane + 1], live.shape)

    def fold(x):
        return jnp.sum(x.reshape(x.shape[0] // SUB, SUB, x.shape[1]), axis=0)

    def correlate(k, _):
        first = jnp.clip(start_ref[k] - me * ch_dev, 0, ch_dev - 1)
        parts = [xw[p, pl.ds(first, tmpl_chans), :] for p in range(panels)]
        row = pl.ds(pl.multiple_of(k * SUB, SUB), SUB)
        for p in range(panels):
            qsum[p, row, :] = fold(parts[p] * parts[p])
        tsum[row, :] = fold(live[pl.ds(first, tmpl_chans), :] * tsq[k])
        data = jnp.concatenate([part.astype(jnp.bfloat16) for part in parts], axis=1)
        acc = jnp.dot(bank_t[k], data, preferred_element_type=jnp.float32)
        half = LANES
        high = acc[half:]
        short = high.shape[0]
        low = jnp.concatenate(
            [acc[:short, : wide - half] + high[:, half:], acc[short:half, : wide - half]], axis=0
        )
        acc = jnp.concatenate([low, acc[:half, wide - half :]], axis=1)
        half //= 2
        acc = (acc[:half] + left(acc[half:], half))[:, :lag_wide]
        while half > SUB:
            half //= 2
            acc = acc[:half] + left(acc[half:], half)
        for p in range(lag_wide // LANES):
            esum[p, row, :] = acc[:, p * LANES : (p + 1) * LANES]
        return 0

    lax.fori_loop(0, tmp_dev, correlate, 0, unroll=4)

    crossed = jnp.zeros((tmp_dev, lag_wide), jnp.float32)
    energy = jnp.zeros((tmp_dev, wide), jnp.float32)
    tmpl_energy = jnp.zeros((tmp_dev, LANES), jnp.float32)
    for b in range(SUB):
        pick = pl.ds(b, tmp_dev, stride=SUB)
        crossed = crossed + left(
            jnp.concatenate([esum[p, pick, :] for p in range(lag_wide // LANES)], axis=1), b
        )
        energy = energy + jnp.concatenate([qsum[p, pick, :] for p in range(panels)], axis=1)
        tmpl_energy = tmpl_energy + tsum[pick, :]
    tmpl_energy = jnp.sum(tmpl_energy, axis=1, keepdims=True)
    box = None
    done = 0
    span = 1
    for bit in range(tmpl_len.bit_length()):
        if tmpl_len & span:
            moved = left(energy, done)
            box = moved if box is None else box + moved
            done += span
        if 2 * span <= tmpl_len:
            energy = energy + left(energy, span)
        span *= 2
    scores = crossed * lax.rsqrt(tmpl_energy * box[:, :lag_wide] + epsilon)
    scores_ref[...] = scores[:, :lag_count]

    pk[me] = jnp.max(scores, axis=0, keepdims=True)

    def swap(d):
        other = lax.rem(me + d, size)
        return pltpu.make_async_remote_copy(
            src_ref=pk.at[me],
            dst_ref=pk.at[me],
            send_sem=pk_send.at[d],
            recv_sem=pk_recv.at[d],
            device_id={"chan": other},
            device_id_type=MESH,
        )

    def swap_start(d, _):
        swap(d).start()
        return 0

    def swap_done(d, _):
        swap(d).wait_recv()
        return 0

    def swap_sent(d, _):
        swap(d).wait_send()
        return 0

    lax.fori_loop(1, size, swap_start, 0)
    lax.fori_loop(1, size, swap_done, 0)
    peaks_ref[...] = jnp.max(pk[...], axis=0)[:, :lag_count]
    lax.fori_loop(1, size, swap_sent, 0)
    for when, copy in sent:

        @pl.when(when)
        def _(copy=copy):
            copy.wait_send()


def local(recording, alive, bank, start):
    ch_dev, length = recording.shape
    tmp_dev, tmpl_chans, tmpl_len = bank.shape
    lag_count = length - tmpl_len + 1
    size = lax.axis_size("chan")
    panels = -(-(length + 1) // LANES)
    rows = up(ch_dev + tmpl_chans - 1, SUB * 2)
    reach = -(-rows // ch_dev) - 1
    lag_wide = up(lag_count + SUB - 1, LANES)
    vmem = pl.BlockSpec(memory_space=pltpu.VMEM)
    anywhere = pl.BlockSpec(memory_space=pl.ANY)
    scores, peaks = pl.pallas_call(
        functools.partial(kernel, size, tmpl_chans, tmpl_len, length, lag_count),
        out_shape=(
            jax.ShapeDtypeStruct((tmp_dev, lag_count), jnp.float32),
            jax.ShapeDtypeStruct((1, lag_count), jnp.float32),
        ),
        in_specs=[pl.BlockSpec(memory_space=pltpu.SMEM), vmem, anywhere, anywhere],
        out_specs=(vmem, vmem),
        scratch_shapes=[
            pltpu.VMEM((length, ch_dev), jnp.float32),
            pltpu.VMEM((LANES, ch_dev), jnp.float32),
            pltpu.VMEM((tmp_dev, tmpl_chans, tmpl_len), bank.dtype),
            pltpu.VMEM((tmp_dev, tmpl_len, tmpl_chans), bank.dtype),
            pltpu.VMEM((tmp_dev, tmpl_chans, LANES), jnp.float32),
            pltpu.VMEM((panels, rows, LANES), jnp.float32),
            pltpu.VMEM((panels, ch_dev, LANES), jnp.float32),
            pltpu.VMEM((rows, LANES), jnp.float32),
            pltpu.VMEM((lag_wide // LANES, tmp_dev * SUB, LANES), jnp.float32),
            pltpu.VMEM((panels, tmp_dev * SUB, LANES), jnp.float32),
            pltpu.VMEM((tmp_dev * SUB, LANES), jnp.float32),
            pltpu.VMEM((size, 1, lag_wide), jnp.float32),
            pltpu.SemaphoreType.DMA(()),
            pltpu.SemaphoreType.DMA((tmp_dev,)),
            pltpu.SemaphoreType.DMA((24,)),
            pltpu.SemaphoreType.DMA((reach, HALVES)),
            pltpu.SemaphoreType.DMA((HALVES,)),
            pltpu.SemaphoreType.DMA((size,)),
            pltpu.SemaphoreType.DMA((size,)),
        ],
        compiler_params=pltpu.CompilerParams(
            collective_id=0, has_side_effects=True, vmem_limit_bytes=60 * 1024 * 1024
        ),
    )(start, alive.reshape(1, ch_dev), recording.T, bank)
    return scores, peaks.reshape(lag_count)


def solution(mesh):
    placed = (
        P(("parts", "chan"), None),
        P(("parts", "chan")),
        P(("parts", "chan"), None, None),
        P(("parts", "chan")),
    )
    return jax.shard_map(
        local,
        mesh=mesh,
        in_specs=placed,
        out_specs=(P(("parts", "chan"), None), P("parts")),
        check_vma=False,
    )
```

```python
import functools

import jax
import jax.numpy as jnp
from jax import lax
from jax.experimental import pallas as pl
from jax.experimental.pallas import tpu as pltpu
from jax.sharding import PartitionSpec as P

epsilon = 1e-06
LANES = 128
SUB = 8
HALVES = 2
MESH = pl.DeviceIdType.MESH


def up(value, unit):
    return -(-value // unit) * unit


def left(x, by):
    by = by % x.shape[-1]
    return x if by == 0 else pltpu.roll(x, x.shape[-1] - by, x.ndim - 1)


def kernel(
    size, tmpl_chans, tmpl_len, length, lag_count,
    start_ref, alive_ref, rec_hbm, bank_hbm,
    out_ref,
    rec_v, turn, bank_v, bank_t, tsq, xw, relay, x2, xb, offv, esum, qsum, pk,
    rec_sem, bank_sem, send_sem, recv_sem, relay_sem, pk_send, pk_recv,
):
    me = lax.axis_index("chan")
    ch_dev = rec_v.shape[1]
    tmp_dev = bank_v.shape[0]
    panels, rows, _ = xw.shape
    wide = panels * LANES
    lag_wide = up(lag_count + SUB - 1, LANES)
    reach = -(-rows // ch_dev) - 1
    tail_lane = length - (panels - 1) * LANES

    barrier = pltpu.get_barrier_semaphore()

    def greet(d, _):
        pl.semaphore_signal(
            barrier, inc=1, device_id={"chan": lax.rem(me + d, size)}, device_id_type=MESH
        )
        return 0

    lax.fori_loop(1, size, greet, 0)

    rec_copy = pltpu.make_async_copy(rec_hbm, rec_v, rec_sem)
    rec_copy.start()
    bank_copies = [
        pltpu.make_async_copy(bank_hbm.at[k], bank_v.at[k], bank_sem.at[k])
        for k in range(tmp_dev)
    ]
    for copy in bank_copies:
        copy.start()

    flags = alive_ref[...].astype(jnp.float32)
    turn[...] = jnp.zeros(turn.shape, jnp.float32)
    turn[tail_lane : tail_lane + 1, :] = flags
    rec_copy.wait()
    for p in range(panels - 1):
        xw[p, :ch_dev, :] = (rec_v[p * LANES : (p + 1) * LANES, :] * flags).T
    turn[:tail_lane, :] = rec_v[(panels - 1) * LANES : length, :] * flags
    xw[panels - 1, :ch_dev, :] = turn[...].T

    pl.semaphore_wait(barrier, size - 1)

    part = ch_dev // HALVES
    role = lax.rem(me, 4)
    further = me >= 4
    sent = []

    def rows_of(slot, h):
        return pl.ds(slot * ch_dev + h * part, part)

    def send(when, src, dst, arrival, by):
        copy = pltpu.make_async_remote_copy(
            src_ref=src,
            dst_ref=dst,
            send_sem=send_sem.at[len(sent)],
            recv_sem=arrival,
            device_id={"chan": lax.rem(me + by + size, size)},
            device_id_type=MESH,
        )
        sent.append((when, copy))

        @pl.when(when)
        def _():
            copy.start()

    def to_slot(when, from_slot, h, slot, by):
        send(
            when,
            xw.at[:, rows_of(from_slot, h), :],
            xw.at[:, rows_of(slot, h), :],
            recv_sem.at[slot - 1, h],
            by,
        )

    def arrived(slot, h):
        where = xw.at[:, pl.ds(slot * ch_dev, tail) if slot == reach else rows_of(slot, h), :]
        pltpu.make_async_remote_copy(
            src_ref=where,
            dst_ref=where,
            send_sem=send_sem.at[0],
            recv_sem=recv_sem.at[slot - 1, h],
            device_id={"chan": lax.rem(me + 1, size)},
            device_id_type=MESH,
        ).wait_recv()

    is_a, is_b, is_c, is_d = (role == r for r in range(4))
    tail = rows - reach * ch_dev
    for h in range(HALVES):
        send(
            is_b & further,
            xw.at[:, rows_of(0, h), :],
            relay.at[:, pl.ds(h * part, part), :],
            relay_sem.at[h],
            2,
        )
        to_slot((is_a | is_c) & further, 0, h, 3, -3)
        to_slot(is_c | is_d, 0, h, 2, -2)
        to_slot(is_b | is_d, 0, h, 1, -1)
    send(
        further,
        xw.at[:, pl.ds(0, tail), :],
        xw.at[:, pl.ds(reach * ch_dev, tail), :],
        recv_sem.at[reach - 1, 0],
        -4,
    )
    for d in range(1, reach + 1):
        count = min(ch_dev, rows - d * ch_dev)

        @pl.when(me + d >= size)
        def _(d=d, count=count):
            xw[:, d * ch_dev : d * ch_dev + count, :] = jnp.zeros(
                (panels, count, LANES), jnp.float32
            )

    def pass_on(when, from_slot, h, slot, by):
        @pl.when(when)
        def _():
            arrived(from_slot, h)

        to_slot(when, from_slot, h, slot, by)

    def pass_back(h):
        when = is_d & further

        @pl.when(when)
        def _():
            where = relay.at[:, pl.ds(h * part, part), :]
            pltpu.make_async_remote_copy(
                src_ref=where,
                dst_ref=where,
                send_sem=send_sem.at[0],
                recv_sem=relay_sem.at[h],
                device_id={"chan": lax.rem(me + 1, size)},
                device_id_type=MESH,
            ).wait_recv()

        send(
            when,
            relay.at[:, pl.ds(h * part, part), :],
            xw.at[:, rows_of(2, h), :],
            recv_sem.at[1, h],
            -4,
        )

    b_in, d_in = is_b & (me + 3 < size), is_d & (me + 1 < size)

    def relay_round(number):
        if number == 0:
            pass_on(b_in, 3, 0, 1, 2)
            pass_back(0)
        elif number == 1:
            pass_on(b_in, 3, 1, 1, 2)
            pass_back(1)
            pass_on(is_a, 2, 0, 1, 1)
            pass_on(is_b, 2, 0, 3, -1)
        elif number == 2:
            pass_on(d_in, 1, 0, 2, -1)
            pass_on(d_in, 2, 0, 3, -1)
        else:
            pass_on(is_a, 2, 1, 1, 1)
            pass_on(is_b, 2, 1, 3, -1)
            pass_on(d_in, 1, 1, 2, -1)
            pass_on(d_in, 2, 1, 3, -1)

    circle = reach * ch_dev
    rings = circle // LANES
    lane_t = lax.broadcasted_iota(jnp.int32, (tmpl_len, LANES), 1)
    row_id = lax.broadcasted_iota(jnp.int32, (ch_dev, LANES), 0)
    for p in range(panels):
        x2[p] = jnp.square(xw[p, :ch_dev, :])

    def offset_of(k):
        return jnp.clip(start_ref[k] - me * ch_dev, 0, ch_dev - 1)

    def fold(x):
        return jnp.sum(x.reshape(x.shape[0] // SUB, SUB, x.shape[1]), axis=0)

    def block_of(k):
        return pl.ds(pl.multiple_of(k * SUB, SUB), SUB)

    def prepare(k, _):
        pltpu.make_async_copy(bank_hbm.at[k], bank_v.at[k], bank_sem.at[k]).wait()
        offset = offset_of(k)
        wide_t = jnp.concatenate(
            [
                bank_v[k].T.astype(jnp.float32),
                jnp.zeros((tmpl_len, circle - tmpl_chans), jnp.float32),
            ],
            axis=1,
        )
        turned = [
            pltpu.roll(wide_t[:, p * LANES : (p + 1) * LANES], offset, 1) for p in range(rings)
        ]
        wraps = lane_t < offset
        for p in range(rings):
            piece = jnp.where(wraps, turned[p - 1], turned[p])
            bank_t[k, :, p * LANES : (p + 1) * LANES] = piece.astype(bank_t.dtype)
            tsq[p, block_of(k), :] = fold(piece * piece)
        offv[block_of(k), :] = jnp.full((SUB, LANES), offset, jnp.int32)
        inside = row_id >= offset
        for p in range(panels):
            qsum[p, block_of(k), :] = fold(jnp.where(inside, x2[p], 0.0))
        return 0

    share = 3 * tmp_dev // 16
    begin = 0
    for number in range(4):
        end = begin + share
        lax.fori_loop(begin, end, prepare, 0, unroll=True)
        relay_round(number)
        begin = end
    lax.fori_loop(begin, tmp_dev, prepare, 0, unroll=True)

    for d in range(1, reach + 1):
        for h in range(HALVES if d < reach else 1):
            waited = {1: d_in, 2: is_a | is_b | d_in, 3: b_in}.get(d)
            here = me + d < size
            if waited is not None:
                here = here & jnp.logical_not(waited)

            @pl.when(here)
            def _(d=d, h=h):
                arrived(d, h)

    for p in range(panels):
        columns = slice(p * LANES, (p + 1) * LANES)
        rounded = xw[p, :circle, :].astype(jnp.bfloat16)
        xb[0, :, columns] = rounded
        xb[1, tail:, columns] = rounded[tail:]
        xb[1, :tail, columns] = xw[p, circle:, :].astype(jnp.bfloat16)
    common = [fold(jnp.square(xw[p, ch_dev:tmpl_chans, :])) for p in range(panels)]
    for p in range(panels):
        x2[p] = jnp.square(xw[p, tmpl_chans : tmpl_chans + ch_dev, :])
    skip = ((panels - 1) * LANES - lag_count + 1) // 16 * 16

    def correlate(k, _):
        offset = offset_of(k)
        inside = row_id < offset
        for p in range(panels):
            qsum[p, block_of(k), :] += common[p] + fold(jnp.where(inside, x2[p], 0.0))
        data = xb.at[(offset + tmpl_chans > circle).astype(jnp.int32)]
        main = panels - 1
        acc = jnp.dot(
            bank_t[k], data[:, : main * LANES], preferred_element_type=jnp.float32
        )
        last = jnp.dot(
            bank_t[k, skip:, :], data[:, main * LANES :], preferred_element_type=jnp.float32
        )
        half = LANES
        high = jnp.concatenate([acc[half:, half:], last[half - skip :]], axis=1)
        acc = jnp.concatenate([acc[: tmpl_len - half] + high, acc[tmpl_len - half : half]], axis=0)
        edge = last[: half - skip]
        half //= 2
        edge = jnp.concatenate(
            [jnp.zeros((half - edge.shape[0], LANES), jnp.float32), edge], axis=0
        )
        high = left(jnp.concatenate([acc[half:], edge], axis=1), half)
        acc = acc[:half] + high[:, : main * LANES]
        while half > SUB:
            half //= 2
            acc = acc[:half] + left(acc[half:], half)
        for p in range(main):
            esum[p, block_of(k), :] = acc[:, p * LANES : (p + 1) * LANES]
        return 0

    lax.fori_loop(0, tmp_dev, correlate, 0, unroll=4)

    crossed = jnp.zeros((tmp_dev, lag_wide), jnp.float32)
    energy = jnp.zeros((tmp_dev, wide), jnp.float32)
    tmpl_rows = [jnp.zeros((tmp_dev, LANES), jnp.float32) for _ in range(rings)]
    for b in range(SUB):
        pick = pl.ds(b, tmp_dev, stride=SUB)
        crossed = crossed + left(
            jnp.concatenate([esum[p, pick, :] for p in range(lag_wide // LANES)], axis=1), b
        )
        energy = energy + jnp.concatenate([qsum[p, pick, :] for p in range(panels)], axis=1)
        tmpl_rows = [tmpl_rows[p] + tsq[p, pick, :] for p in range(rings)]
    def on_lanes(first, count):
        flag = xw[panels - 1, first : first + count, tail_lane : tail_lane + 1]
        spot = lax.broadcasted_iota(jnp.int32, (count, LANES), 0) == lax.broadcasted_iota(
            jnp.int32, (count, LANES), 1
        )
        return jnp.sum(jnp.where(spot, flag, 0.0), axis=0, keepdims=True)

    live = [on_lanes(p * LANES, LANES) for p in range(rings)]
    lane_k = lax.broadcasted_iota(jnp.int32, (tmp_dev, LANES), 1)
    wrapped = (offv[pl.ds(0, tmp_dev, stride=SUB), :] + tmpl_chans > circle) & (lane_k < tail)
    tmpl_energy = tmpl_rows[0] * jnp.where(wrapped, on_lanes(circle, tail), live[0])
    for p in range(1, rings):
        tmpl_energy = tmpl_energy + tmpl_rows[p] * live[p]
    tmpl_energy = jnp.sum(tmpl_energy, axis=1, keepdims=True)
    box = None
    done = 0
    span = 1
    for bit in range(tmpl_len.bit_length()):
        if tmpl_len & span:
            moved = left(energy, done)
            box = moved if box is None else box + moved
            done += span
        if 2 * span <= tmpl_len:
            energy = energy + left(energy, span)
        span *= 2
    scores = crossed * lax.rsqrt(tmpl_energy * box[:, :lag_wide] + epsilon)
    out_ref[:tmp_dev, :] = scores[:, :lag_count]

    pk[me] = jnp.max(scores, axis=0, keepdims=True)

    def swap(d):
        other = lax.rem(me + d, size)
        return pltpu.make_async_remote_copy(
            src_ref=pk.at[me],
            dst_ref=pk.at[me],
            send_sem=pk_send.at[d],
            recv_sem=pk_recv.at[d],
            device_id={"chan": other},
            device_id_type=MESH,
        )

    def swap_start(d, _):
        swap(d).start()
        return 0

    def swap_done(d, _):
        swap(d).wait_recv()
        return 0

    def swap_sent(d, _):
        swap(d).wait_send()
        return 0

    lax.fori_loop(1, size, swap_start, 0)
    lax.fori_loop(1, size, swap_done, 0)
    out_ref[tmp_dev : tmp_dev + 1, :] = jnp.max(pk[...], axis=0)[:, :lag_count]
    lax.fori_loop(1, size, swap_sent, 0)
    for when, copy in sent:

        @pl.when(when)
        def _(copy=copy):
            copy.wait_send()


def local(recording, alive, bank, start):
    ch_dev, length = recording.shape
    tmp_dev, tmpl_chans, tmpl_len = bank.shape
    lag_count = length - tmpl_len + 1
    size = lax.axis_size("chan")
    panels = -(-(length + 1) // LANES)
    rows = up(ch_dev + tmpl_chans - 1, SUB * 2)
    reach = -(-rows // ch_dev) - 1
    lag_wide = up(lag_count + SUB - 1, LANES)
    vmem = pl.BlockSpec(memory_space=pltpu.VMEM)
    anywhere = pl.BlockSpec(memory_space=pl.ANY)
    out = pl.pallas_call(
        functools.partial(kernel, size, tmpl_chans, tmpl_len, length, lag_count),
        out_shape=jax.ShapeDtypeStruct((tmp_dev + 1, lag_count), jnp.float32),
        in_specs=[pl.BlockSpec(memory_space=pltpu.SMEM), vmem, anywhere, anywhere],
        out_specs=vmem,
        scratch_shapes=[
            pltpu.VMEM((length, ch_dev), jnp.float32),
            pltpu.VMEM((LANES, ch_dev), jnp.float32),
            pltpu.VMEM((tmp_dev, tmpl_chans, tmpl_len), bank.dtype),
            pltpu.VMEM((tmp_dev, tmpl_len, reach * ch_dev), bank.dtype),
            pltpu.VMEM((reach * ch_dev // LANES, tmp_dev * SUB, LANES), jnp.float32),
            pltpu.VMEM((panels, rows, LANES), jnp.float32),
            pltpu.VMEM((panels, ch_dev, LANES), jnp.float32),
            pltpu.VMEM((panels, ch_dev, LANES), jnp.float32),
            pltpu.VMEM((2, reach * ch_dev, panels * LANES), jnp.bfloat16),
            pltpu.VMEM((tmp_dev * SUB, LANES), jnp.int32),
            pltpu.VMEM((lag_wide // LANES, tmp_dev * SUB, LANES), jnp.float32),
            pltpu.VMEM((panels, tmp_dev * SUB, LANES), jnp.float32),
            pltpu.VMEM((size, 1, lag_wide), jnp.float32),
            pltpu.SemaphoreType.DMA(()),
            pltpu.SemaphoreType.DMA((tmp_dev,)),
            pltpu.SemaphoreType.DMA((24,)),
            pltpu.SemaphoreType.DMA((reach, HALVES)),
            pltpu.SemaphoreType.DMA((HALVES,)),
            pltpu.SemaphoreType.DMA((size,)),
            pltpu.SemaphoreType.DMA((size,)),
        ],
        compiler_params=pltpu.CompilerParams(
            collective_id=0, has_side_effects=True, vmem_limit_bytes=60 * 1024 * 1024
        ),
    )(start, alive.reshape(1, ch_dev), recording.T, bank)
    return out[:tmp_dev], out[tmp_dev]


def solution(mesh):
    placed = (
        P(("parts", "chan"), None),
        P(("parts", "chan")),
        P(("parts", "chan"), None, None),
        P(("parts", "chan")),
    )
    return jax.shard_map(
        local,
        mesh=mesh,
        in_specs=placed,
        out_specs=(P(("parts", "chan"), None), P("parts")),
        check_vma=False,
    )
```

```python
import functools

import jax
import jax.numpy as jnp
from jax import lax
from jax.experimental import pallas as pl
from jax.experimental.pallas import tpu as pltpu
from jax.sharding import PartitionSpec as P

epsilon = 1e-06
LANES = 128
SUB = 8
HALVES = 2
MESH = pl.DeviceIdType.MESH


def up(value, unit):
    return -(-value // unit) * unit


def left(x, by):
    by = by % x.shape[-1]
    return x if by == 0 else pltpu.roll(x, x.shape[-1] - by, x.ndim - 1)


def kernel(
    size, tmpl_chans, tmpl_len, length, lag_count,
    start_ref, alive_ref, rec_hbm, bank_hbm,
    scores_ref, peaks_ref,
    rec_v, turn, bank_v, bank_t, tsq, xw, relay, x2, xb, offv, esum, qsum, pk,
    rec_sem, bank_sem, send_sem, recv_sem, relay_sem, pk_send, pk_recv,
):
    me = lax.axis_index("chan")
    ch_dev = rec_v.shape[1]
    tmp_dev = bank_v.shape[0]
    panels, rows, _ = xw.shape
    wide = panels * LANES
    lag_wide = up(lag_count + SUB - 1, LANES)
    reach = -(-rows // ch_dev) - 1
    tail_lane = length - (panels - 1) * LANES

    barrier = pltpu.get_barrier_semaphore()

    def greet(d, _):
        pl.semaphore_signal(
            barrier, inc=1, device_id={"chan": lax.rem(me + d, size)}, device_id_type=MESH
        )
        return 0

    lax.fori_loop(1, size, greet, 0)

    rec_copy = pltpu.make_async_copy(rec_hbm, rec_v, rec_sem)
    rec_copy.start()
    bank_copies = [
        pltpu.make_async_copy(bank_hbm.at[k], bank_v.at[k], bank_sem.at[k])
        for k in range(tmp_dev)
    ]
    for copy in bank_copies:
        copy.start()

    flags = alive_ref[...].astype(jnp.float32)
    turn[...] = jnp.zeros(turn.shape, jnp.float32)
    turn[tail_lane : tail_lane + 1, :] = flags
    rec_copy.wait()
    for p in range(panels - 1):
        xw[p, :ch_dev, :] = (rec_v[p * LANES : (p + 1) * LANES, :] * flags).T
    turn[:tail_lane, :] = rec_v[(panels - 1) * LANES : length, :] * flags
    xw[panels - 1, :ch_dev, :] = turn[...].T

    pl.semaphore_wait(barrier, size - 1)

    part = ch_dev // HALVES
    role = lax.rem(me, 4)
    further = me >= 4
    sent = []

    def rows_of(slot, h):
        return pl.ds(slot * ch_dev + h * part, part)

    def send(when, src, dst, arrival, by):
        copy = pltpu.make_async_remote_copy(
            src_ref=src,
            dst_ref=dst,
            send_sem=send_sem.at[len(sent)],
            recv_sem=arrival,
            device_id={"chan": lax.rem(me + by + size, size)},
            device_id_type=MESH,
        )
        sent.append((when, src))

        @pl.when(when)
        def _():
            copy.start()

    def to_slot(when, from_slot, h, slot, by):
        send(
            when,
            xw.at[:, rows_of(from_slot, h), :],
            xw.at[:, rows_of(slot, h), :],
            recv_sem.at[slot - 1, h],
            by,
        )

    def arrived(slot, h):
        where = xw.at[:, pl.ds(slot * ch_dev, tail) if slot == reach else rows_of(slot, h), :]
        pltpu.make_async_remote_copy(
            src_ref=where,
            dst_ref=where,
            send_sem=send_sem.at[0],
            recv_sem=recv_sem.at[slot - 1, h],
            device_id={"chan": lax.rem(me + 1, size)},
            device_id_type=MESH,
        ).wait_recv()

    is_a, is_b, is_c, is_d = (role == r for r in range(4))
    tail = rows - reach * ch_dev
    for h in range(HALVES):
        send(
            is_b & further,
            xw.at[:, rows_of(0, h), :],
            relay.at[:, pl.ds(h * part, part), :],
            relay_sem.at[h],
            2,
        )
        to_slot((is_a | is_c) & further, 0, h, 3, -3)
        to_slot(is_c | is_d, 0, h, 2, -2)
        to_slot(is_b | is_d, 0, h, 1, -1)
    send(
        further,
        xw.at[:, pl.ds(0, tail), :],
        xw.at[:, pl.ds(reach * ch_dev, tail), :],
        recv_sem.at[reach - 1, 0],
        -4,
    )
    for d in range(1, reach + 1):
        count = min(ch_dev, rows - d * ch_dev)

        @pl.when(me + d >= size)
        def _(d=d, count=count):
            xw[:, d * ch_dev : d * ch_dev + count, :] = jnp.zeros(
                (panels, count, LANES), jnp.float32
            )

    def pass_on(when, from_slot, h, slot, by):
        @pl.when(when)
        def _():
            arrived(from_slot, h)

        to_slot(when, from_slot, h, slot, by)

    def pass_back(h):
        when = back

        @pl.when(when)
        def _():
            where = relay.at[:, pl.ds(h * part, part), :]
            pltpu.make_async_remote_copy(
                src_ref=where,
                dst_ref=where,
                send_sem=send_sem.at[0],
                recv_sem=relay_sem.at[h],
                device_id={"chan": lax.rem(me + 1, size)},
                device_id_type=MESH,
            ).wait_recv()

        send(
            when,
            relay.at[:, pl.ds(h * part, part), :],
            xw.at[:, rows_of(2, h), :],
            recv_sem.at[1, h],
            -4,
        )

    back = is_d & further
    b_in, d_in = is_b & (me + 3 < size), is_d & (me + 1 < size)

    def relay_round(number):
        if number == 0:
            pass_on(b_in, 3, 0, 1, 2)
            pass_back(0)
        elif number == 1:
            pass_on(b_in, 3, 1, 1, 2)
            pass_back(1)
            pass_on(is_a, 2, 0, 1, 1)
            pass_on(is_b, 2, 0, 3, -1)
        elif number == 2:
            pass_on(d_in, 1, 0, 2, -1)
            pass_on(d_in, 2, 0, 3, -1)
        else:
            pass_on(is_a, 2, 1, 1, 1)
            pass_on(is_b, 2, 1, 3, -1)
            pass_on(d_in, 1, 1, 2, -1)
            pass_on(d_in, 2, 1, 3, -1)

    circle = reach * ch_dev
    rings = circle // LANES
    lane_t = lax.broadcasted_iota(jnp.int32, (tmpl_len, LANES), 1)
    row_id = lax.broadcasted_iota(jnp.int32, (ch_dev, LANES), 0)
    for p in range(panels):
        x2[p] = jnp.square(xw[p, :ch_dev, :])

    eye = (
        lax.broadcasted_iota(jnp.int32, (tmpl_len, tmpl_len), 0)
        == lax.broadcasted_iota(jnp.int32, (tmpl_len, tmpl_len), 1)
    ).astype(bank_v.dtype)

    def offset_of(k):
        return jnp.clip(start_ref[k] - me * ch_dev, 0, ch_dev - 1)

    def fold(x):
        return jnp.sum(x.reshape(x.shape[0] // SUB, SUB, x.shape[1]), axis=0)

    def block_of(k):
        return pl.ds(pl.multiple_of(k * SUB, SUB), SUB)

    def prepare(k, _):
        pltpu.make_async_copy(bank_hbm.at[k], bank_v.at[k], bank_sem.at[k]).wait()
        offset = offset_of(k)
        wide_t = jnp.concatenate(
            [
                lax.dot_general(
                    eye,
                    bank_v[k],
                    (((1,), (1,)), ((), ())),
                    preferred_element_type=jnp.float32,
                ),
                jnp.zeros((tmpl_len, circle - tmpl_chans), jnp.float32),
            ],
            axis=1,
        )
        turned = [
            pltpu.roll(wide_t[:, p * LANES : (p + 1) * LANES], offset, 1) for p in range(rings)
        ]
        wraps = lane_t < offset
        for p in range(rings):
            piece = jnp.where(wraps, turned[p - 1], turned[p])
            bank_t[k, :, p * LANES : (p + 1) * LANES] = piece.astype(bank_t.dtype)
            tsq[p, block_of(k), :] = fold(piece * piece)
        offv[block_of(k), :] = jnp.full((SUB, LANES), offset, jnp.int32)
        inside = row_id >= offset
        for p in range(panels):
            qsum[p, block_of(k), :] = fold(jnp.where(inside, x2[p], 0.0))
        return 0

    def prepare_some(j, _):
        for u in range(2):
            prepare(2 * j + u, 0)
        for number, after in enumerate((1, 3, 4, 6)):

            @pl.when(j == after)
            def _(number=number):
                relay_round(number)

        return 0

    lax.fori_loop(0, tmp_dev // 2, prepare_some, 0)

    for d in range(1, reach + 1):
        for h in range(HALVES if d < reach else 1):
            waited = {1: d_in, 2: is_a | is_b | d_in, 3: b_in}.get(d)
            here = me + d < size
            if waited is not None:
                here = here & jnp.logical_not(waited)

            @pl.when(here)
            def _(d=d, h=h):
                arrived(d, h)

    for p in range(panels):
        columns = slice(p * LANES, (p + 1) * LANES)
        rounded = xw[p, :circle, :].astype(jnp.bfloat16)
        xb[0, :, columns] = rounded
        xb[1, tail:, columns] = rounded[tail:]
        xb[1, :tail, columns] = xw[p, circle:, :].astype(jnp.bfloat16)
    common = [fold(jnp.square(xw[p, ch_dev:tmpl_chans, :])) for p in range(panels)]
    for p in range(panels):
        x2[p] = jnp.square(xw[p, tmpl_chans : tmpl_chans + ch_dev, :])
    skip = ((panels - 1) * LANES - lag_count + 1) // 16 * 16

    def correlate(k, _):
        offset = offset_of(k)
        inside = row_id < offset
        for p in range(panels):
            qsum[p, block_of(k), :] += common[p] + fold(jnp.where(inside, x2[p], 0.0))
        data = xb.at[(offset + tmpl_chans > circle).astype(jnp.int32)]
        main = panels - 1
        acc = jnp.dot(
            bank_t[k], data[:, : main * LANES], preferred_element_type=jnp.float32
        )
        last = jnp.dot(
            bank_t[k, skip:, :], data[:, main * LANES :], preferred_element_type=jnp.float32
        )
        half = LANES
        high = jnp.concatenate([acc[half:, half:], last[half - skip :]], axis=1)
        acc = jnp.concatenate([acc[: tmpl_len - half] + high, acc[tmpl_len - half : half]], axis=0)
        edge = last[: half - skip]
        half //= 2
        edge = jnp.concatenate(
            [jnp.zeros((half - edge.shape[0], LANES), jnp.float32), edge], axis=0
        )
        high = left(jnp.concatenate([acc[half:], edge], axis=1), half)
        acc = acc[:half] + high[:, : main * LANES]
        while half > SUB:
            half //= 2
            acc = acc[:half] + left(acc[half:], half)
        for p in range(main):
            esum[p, block_of(k), :] = acc[:, p * LANES : (p + 1) * LANES]
        return 0

    lax.fori_loop(0, tmp_dev, correlate, 0, unroll=4)

    crossed = jnp.zeros((tmp_dev, lag_wide), jnp.float32)
    energy = jnp.zeros((tmp_dev, wide), jnp.float32)
    tmpl_rows = [jnp.zeros((tmp_dev, LANES), jnp.float32) for _ in range(rings)]
    for b in range(SUB):
        pick = pl.ds(b, tmp_dev, stride=SUB)
        crossed = crossed + left(
            jnp.concatenate([esum[p, pick, :] for p in range(lag_wide // LANES)], axis=1), b
        )
        energy = energy + jnp.concatenate([qsum[p, pick, :] for p in range(panels)], axis=1)
        tmpl_rows = [tmpl_rows[p] + tsq[p, pick, :] for p in range(rings)]
    def on_lanes(first, count):
        flag = xw[panels - 1, first : first + count, tail_lane : tail_lane + 1]
        spot = lax.broadcasted_iota(jnp.int32, (count, LANES), 0) == lax.broadcasted_iota(
            jnp.int32, (count, LANES), 1
        )
        return jnp.sum(jnp.where(spot, flag, 0.0), axis=0, keepdims=True)

    live = [on_lanes(p * LANES, LANES) for p in range(rings)]
    lane_k = lax.broadcasted_iota(jnp.int32, (tmp_dev, LANES), 1)
    wrapped = (offv[pl.ds(0, tmp_dev, stride=SUB), :] + tmpl_chans > circle) & (lane_k < tail)
    tmpl_energy = tmpl_rows[0] * jnp.where(wrapped, on_lanes(circle, tail), live[0])
    for p in range(1, rings):
        tmpl_energy = tmpl_energy + tmpl_rows[p] * live[p]
    tmpl_energy = jnp.sum(tmpl_energy, axis=1, keepdims=True)
    box = None
    done = 0
    span = 1
    for bit in range(tmpl_len.bit_length()):
        if tmpl_len & span:
            moved = left(energy, done)
            box = moved if box is None else box + moved
            done += span
        if 2 * span <= tmpl_len:
            energy = energy + left(energy, span)
        span *= 2
    scores = crossed * lax.rsqrt(tmpl_energy * box[:, :lag_wide] + epsilon)
    scores_ref[...] = scores[:, :lag_count]

    pk[me] = jnp.max(scores, axis=0, keepdims=True)

    def swap(d):
        other = lax.rem(me + d, size)
        return pltpu.make_async_remote_copy(
            src_ref=pk.at[me],
            dst_ref=pk.at[me],
            send_sem=pk_send.at[d],
            recv_sem=pk_recv.at[d],
            device_id={"chan": other},
            device_id_type=MESH,
        )

    def swap_start(d, _):
        swap(d).start()
        return 0

    def swap_done(d, _):
        swap(d).wait_recv()
        return 0

    def swap_sent(d, _):
        swap(d).wait_send()
        return 0

    lax.fori_loop(1, size, swap_start, 0)
    lax.fori_loop(1, size, swap_done, 0)
    peaks_ref[...] = jnp.max(pk[...], axis=0)[:, :lag_count]
    lax.fori_loop(1, size, swap_sent, 0)
    for number, (when, src) in enumerate(sent):

        @pl.when(when)
        def _(number=number, src=src):
            pltpu.make_async_remote_copy(
                src_ref=src,
                dst_ref=src,
                send_sem=send_sem.at[number],
                recv_sem=recv_sem.at[0, 0],
                device_id={"chan": lax.rem(me + 1, size)},
                device_id_type=MESH,
            ).wait_send()


def hand_out(scores_in, peaks_in, scores_out, peaks_out, sems):
    copies = [
        pltpu.make_async_copy(scores_in, scores_out, sems.at[0]),
        pltpu.make_async_copy(peaks_in, peaks_out, sems.at[1]),
    ]
    for copy in copies:
        copy.start()
    for copy in copies:
        copy.wait()


def local(recording, alive, bank, start):
    ch_dev, length = recording.shape
    tmp_dev, tmpl_chans, tmpl_len = bank.shape
    lag_count = length - tmpl_len + 1
    size = lax.axis_size("chan")
    panels = -(-(length + 1) // LANES)
    rows = up(ch_dev + tmpl_chans - 1, SUB * 2)
    reach = -(-rows // ch_dev) - 1
    lag_wide = up(lag_count + SUB - 1, LANES)
    vmem = pl.BlockSpec(memory_space=pltpu.VMEM)
    anywhere = pl.BlockSpec(memory_space=pl.ANY)
    results = (
        jax.ShapeDtypeStruct((tmp_dev, lag_count), jnp.float32),
        jax.ShapeDtypeStruct((1, lag_count), jnp.float32),
    )
    scores, peaks = pl.pallas_call(
        functools.partial(kernel, size, tmpl_chans, tmpl_len, length, lag_count),
        out_shape=results,
        in_specs=[pl.BlockSpec(memory_space=pltpu.SMEM), vmem, anywhere, anywhere],
        out_specs=(vmem, vmem),
        scratch_shapes=[
            pltpu.VMEM((length, ch_dev), jnp.float32),
            pltpu.VMEM((LANES, ch_dev), jnp.float32),
            pltpu.VMEM((tmp_dev, tmpl_chans, tmpl_len), bank.dtype),
            pltpu.VMEM((tmp_dev, tmpl_len, reach * ch_dev), bank.dtype),
            pltpu.VMEM((reach * ch_dev // LANES, tmp_dev * SUB, LANES), jnp.float32),
            pltpu.VMEM((panels, rows, LANES), jnp.float32),
            pltpu.VMEM((panels, ch_dev, LANES), jnp.float32),
            pltpu.VMEM((panels, ch_dev, LANES), jnp.float32),
            pltpu.VMEM((2, reach * ch_dev, panels * LANES), jnp.bfloat16),
            pltpu.VMEM((tmp_dev * SUB, LANES), jnp.int32),
            pltpu.VMEM((lag_wide // LANES, tmp_dev * SUB, LANES), jnp.float32),
            pltpu.VMEM((panels, tmp_dev * SUB, LANES), jnp.float32),
            pltpu.VMEM((size, 1, lag_wide), jnp.float32),
            pltpu.SemaphoreType.DMA(()),
            pltpu.SemaphoreType.DMA((tmp_dev,)),
            pltpu.SemaphoreType.DMA((24,)),
            pltpu.SemaphoreType.DMA((reach, HALVES)),
            pltpu.SemaphoreType.DMA((HALVES,)),
            pltpu.SemaphoreType.DMA((size,)),
            pltpu.SemaphoreType.DMA((size,)),
        ],
        compiler_params=pltpu.CompilerParams(
            collective_id=0, has_side_effects=True, vmem_limit_bytes=60 * 1024 * 1024
        ),
    )(start, alive.reshape(1, ch_dev), recording.T, bank)
    scores, peaks = pl.pallas_call(
        hand_out,
        out_shape=results,
        in_specs=[anywhere, anywhere],
        out_specs=(anywhere, anywhere),
        scratch_shapes=[pltpu.SemaphoreType.DMA((2,))],
        compiler_params=pltpu.CompilerParams(vmem_limit_bytes=60 * 1024 * 1024),
    )(scores, peaks)
    return scores, peaks.reshape(lag_count)


def solution(mesh):
    placed = (
        P(("parts", "chan"), None),
        P(("parts", "chan")),
        P(("parts", "chan"), None, None),
        P(("parts", "chan")),
    )
    return jax.shard_map(
        local,
        mesh=mesh,
        in_specs=placed,
        out_specs=(P(("parts", "chan"), None), P("parts")),
        check_vma=False,
    )
```

```python
import functools

import jax
import jax.numpy as jnp
from jax import lax
from jax.experimental import pallas as pl
from jax.experimental.pallas import tpu as pltpu
from jax.sharding import PartitionSpec as P

epsilon = 1e-06
LANES = 128
SUB = 8
HALVES = 2
GROUP = 4
MESH = pl.DeviceIdType.MESH


def up(value, unit):
    return -(-value // unit) * unit


def left(x, by):
    by = by % x.shape[-1]
    return x if by == 0 else pltpu.roll(x, x.shape[-1] - by, x.ndim - 1)


def kernel(
    size, tmpl_chans, tmpl_len, length, lag_count,
    start_ref, alive_ref, rec_hbm, bank_hbm,
    scores_ref, peaks_ref,
    rec_v, turn, bank_v, bank_t, tsq, xw, relay, x2, xb, esum, qsum, pk,
    rec_sem, bank_sem, send_sem, recv_sem, relay_sem, pk_send, pk_recv,
):
    me = lax.axis_index("chan")
    ch_dev = rec_v.shape[1]
    tmp_dev = bank_v.shape[0]
    panels, rows, _ = xw.shape
    wide = panels * LANES
    lag_wide = up(lag_count + SUB - 1, LANES)
    reach = -(-rows // ch_dev) - 1
    tail_lane = length - (panels - 1) * LANES

    barrier = pltpu.get_barrier_semaphore()

    def greet(d, _):
        pl.semaphore_signal(
            barrier, inc=1, device_id={"chan": lax.rem(me + d, size)}, device_id_type=MESH
        )
        return 0

    lax.fori_loop(1, size, greet, 0)

    rec_copy = pltpu.make_async_copy(rec_hbm, rec_v, rec_sem)
    rec_copy.start()
    bank_copies = [
        pltpu.make_async_copy(bank_hbm.at[k], bank_v.at[k], bank_sem.at[k])
        for k in range(tmp_dev)
    ]
    for copy in bank_copies:
        copy.start()

    flags = alive_ref[...].astype(jnp.float32)
    turn[...] = jnp.zeros(turn.shape, jnp.float32)
    turn[tail_lane : tail_lane + 1, :] = flags
    rec_copy.wait()
    for p in range(panels - 1):
        xw[p, :ch_dev, :] = (rec_v[p * LANES : (p + 1) * LANES, :] * flags).T
    turn[:tail_lane, :] = rec_v[(panels - 1) * LANES : length, :] * flags
    xw[panels - 1, :ch_dev, :] = turn[...].T

    pl.semaphore_wait(barrier, size - 1)

    part = ch_dev // HALVES
    role = lax.rem(me, 4)
    further = me >= 4
    sent = []

    def rows_of(slot, h):
        return pl.ds(slot * ch_dev + h * part, part)

    def send(when, src, dst, arrival, by):
        copy = pltpu.make_async_remote_copy(
            src_ref=src,
            dst_ref=dst,
            send_sem=send_sem.at[len(sent)],
            recv_sem=arrival,
            device_id={"chan": lax.rem(me + by + size, size)},
            device_id_type=MESH,
        )
        sent.append((when, src))

        @pl.when(when)
        def _():
            copy.start()

    def to_slot(when, from_slot, h, slot, by):
        send(
            when,
            xw.at[:, rows_of(from_slot, h), :],
            xw.at[:, rows_of(slot, h), :],
            recv_sem.at[slot - 1, h],
            by,
        )

    def arrived(slot, h):
        where = xw.at[:, pl.ds(slot * ch_dev, tail) if slot == reach else rows_of(slot, h), :]
        pltpu.make_async_remote_copy(
            src_ref=where,
            dst_ref=where,
            send_sem=send_sem.at[0],
            recv_sem=recv_sem.at[slot - 1, h],
            device_id={"chan": lax.rem(me + 1, size)},
            device_id_type=MESH,
        ).wait_recv()

    is_a, is_b, is_c, is_d = (role == r for r in range(4))
    tail = rows - reach * ch_dev
    for h in range(HALVES):
        send(
            is_b & further,
            xw.at[:, rows_of(0, h), :],
            relay.at[:, pl.ds(h * part, part), :],
            relay_sem.at[h],
            2,
        )
        to_slot((is_a | is_c) & further, 0, h, 3, -3)
        to_slot(is_c | is_d, 0, h, 2, -2)
        to_slot(is_b | is_d, 0, h, 1, -1)
    send(
        further,
        xw.at[:, pl.ds(0, tail), :],
        xw.at[:, pl.ds(reach * ch_dev, tail), :],
        recv_sem.at[reach - 1, 0],
        -4,
    )
    for d in range(1, reach + 1):
        count = min(ch_dev, rows - d * ch_dev)

        @pl.when(me + d >= size)
        def _(d=d, count=count):
            xw[:, d * ch_dev : d * ch_dev + count, :] = jnp.zeros(
                (panels, count, LANES), jnp.float32
            )

    def pass_on(when, from_slot, h, slot, by):
        @pl.when(when)
        def _():
            arrived(from_slot, h)

        to_slot(when, from_slot, h, slot, by)

    def pass_back(h):
        when = back

        @pl.when(when)
        def _():
            where = relay.at[:, pl.ds(h * part, part), :]
            pltpu.make_async_remote_copy(
                src_ref=where,
                dst_ref=where,
                send_sem=send_sem.at[0],
                recv_sem=relay_sem.at[h],
                device_id={"chan": lax.rem(me + 1, size)},
                device_id_type=MESH,
            ).wait_recv()

        send(
            when,
            relay.at[:, pl.ds(h * part, part), :],
            xw.at[:, rows_of(2, h), :],
            recv_sem.at[1, h],
            -4,
        )

    back = is_d & further
    b_in, d_in = is_b & (me + 3 < size), is_d & (me + 1 < size)

    def relay_round(number):
        if number == 0:
            pass_on(b_in, 3, 0, 1, 2)
            pass_back(0)
        elif number == 1:
            pass_on(b_in, 3, 1, 1, 2)
            pass_back(1)
            pass_on(is_a, 2, 0, 1, 1)
            pass_on(is_b, 2, 0, 3, -1)
        elif number == 2:
            pass_on(d_in, 1, 0, 2, -1)
            pass_on(d_in, 2, 0, 3, -1)
        else:
            pass_on(is_a, 2, 1, 1, 1)
            pass_on(is_b, 2, 1, 3, -1)
            pass_on(d_in, 1, 1, 2, -1)
            pass_on(d_in, 2, 1, 3, -1)

    circle = reach * ch_dev
    rings = circle // LANES
    lane_t = lax.broadcasted_iota(jnp.int32, (tmpl_len, LANES), 1)
    row_id = lax.broadcasted_iota(jnp.int32, (ch_dev, LANES), 0)
    for p in range(panels):
        x2[p] = jnp.square(xw[p, :ch_dev, :])

    eye = (
        lax.broadcasted_iota(jnp.int32, (tmpl_len, tmpl_len), 0)
        == lax.broadcasted_iota(jnp.int32, (tmpl_len, tmpl_len), 1)
    ).astype(bank_v.dtype)

    def offset_of(k):
        return jnp.clip(start_ref[k] - me * ch_dev, 0, ch_dev - 1)

    def fold(x):
        return jnp.sum(x.reshape(x.shape[0] // SUB, SUB, x.shape[1]), axis=0)

    def block_of(k):
        return pl.ds(pl.multiple_of(k * SUB, SUB), SUB)

    def prepare(k, _):
        pltpu.make_async_copy(bank_hbm.at[k], bank_v.at[k], bank_sem.at[k]).wait()
        offset = offset_of(k)
        wide_t = jnp.concatenate(
            [
                lax.dot_general(
                    eye,
                    bank_v[k],
                    (((1,), (1,)), ((), ())),
                    preferred_element_type=jnp.float32,
                ),
                jnp.zeros((tmpl_len, circle - tmpl_chans), jnp.float32),
            ],
            axis=1,
        )
        turned = [
            pltpu.roll(wide_t[:, p * LANES : (p + 1) * LANES], offset, 1) for p in range(rings)
        ]
        wraps = lane_t < offset
        for p in range(rings + 1):
            piece = jnp.where(
                wraps, turned[p - 1] if p else 0.0, turned[p] if p < rings else 0.0
            )
            tsq[p, block_of(k), :] = fold(piece * piece)
            lanes = min(LANES, rows - p * LANES)
            bank_t[k, :tmpl_len, p * LANES : p * LANES + lanes] = piece[:, :lanes].astype(
                bank_t.dtype
            )
        inside = row_id >= offset
        for p in range(panels):
            qsum[p, block_of(k), :] = fold(jnp.where(inside, x2[p], 0.0))
        return 0

    def prepare_some(j, _):
        for u in range(2):
            prepare(2 * j + u, 0)
        for number, after in enumerate((1, 3, 4, 6)):

            @pl.when(j == after)
            def _(number=number):
                relay_round(number)

        return 0

    lax.fori_loop(0, tmp_dev // 2, prepare_some, 0)

    for d in range(1, reach + 1):
        for h in range(HALVES if d < reach else 1):
            waited = {1: d_in, 2: is_a | is_b | d_in, 3: b_in}.get(d)
            here = me + d < size
            if waited is not None:
                here = here & jnp.logical_not(waited)

            @pl.when(here)
            def _(d=d, h=h):
                arrived(d, h)

    for p in range(panels):
        xb[:, p * LANES : (p + 1) * LANES] = xw[p].astype(jnp.bfloat16)
    common = [fold(jnp.square(xw[p, ch_dev:tmpl_chans, :])) for p in range(panels)]
    for p in range(panels):
        x2[p] = jnp.square(xw[p, tmpl_chans : tmpl_chans + ch_dev, :])
    skip = ((panels - 1) * LANES - lag_count + 1) // 16 * 16

    main = panels - 1
    tall = bank_t.shape[1]

    def sum_diagonals(k, acc, last):
        half = LANES
        high = jnp.concatenate([acc[half:, half:], last[half - skip :]], axis=1)
        acc = jnp.concatenate([acc[: tmpl_len - half] + high, acc[tmpl_len - half : half]], axis=0)
        edge = last[: half - skip]
        half //= 2
        edge = jnp.concatenate(
            [jnp.zeros((half - edge.shape[0], LANES), jnp.float32), edge], axis=0
        )
        high = left(jnp.concatenate([acc[half:], edge], axis=1), half)
        acc = acc[:half] + high[:, : main * LANES]
        while half > SUB:
            half //= 2
            acc = acc[:half] + left(acc[half:], half)
        for p in range(main):
            esum[p, block_of(k), :] = acc[:, p * LANES : (p + 1) * LANES]

    def correlate(g, _):
        group = pl.ds(g * GROUP, GROUP)
        accs = jnp.dot(
            bank_t[group].reshape(GROUP * tall, rows),
            xb[:, : main * LANES],
            preferred_element_type=jnp.float32,
        )
        lasts = jnp.dot(
            bank_t[group, skip:, :].reshape(GROUP * (tall - skip), rows),
            xb[:, main * LANES :],
            preferred_element_type=jnp.float32,
        )
        for u in range(GROUP):
            k = g * GROUP + u
            inside = row_id < offset_of(k)
            for p in range(panels):
                qsum[p, block_of(k), :] += common[p] + fold(jnp.where(inside, x2[p], 0.0))
            start = u * (tall - skip)
            sum_diagonals(
                k,
                accs[u * tall : u * tall + tmpl_len],
                lasts[start : start + tmpl_len - skip],
            )
        return 0

    lax.fori_loop(0, tmp_dev // GROUP, correlate, 0)

    crossed = jnp.zeros((tmp_dev, lag_wide), jnp.float32)
    energy = jnp.zeros((tmp_dev, wide), jnp.float32)
    tmpl_rows = [jnp.zeros((tmp_dev, LANES), jnp.float32) for _ in range(rings + 1)]
    for b in range(SUB):
        pick = pl.ds(b, tmp_dev, stride=SUB)
        crossed = crossed + left(
            jnp.concatenate([esum[p, pick, :] for p in range(lag_wide // LANES)], axis=1), b
        )
        energy = energy + jnp.concatenate([qsum[p, pick, :] for p in range(panels)], axis=1)
        tmpl_rows = [tmpl_rows[p] + tsq[p, pick, :] for p in range(rings + 1)]
    def on_lanes(first, count):
        flag = xw[panels - 1, first : first + count, tail_lane : tail_lane + 1]
        spot = lax.broadcasted_iota(jnp.int32, (count, LANES), 0) == lax.broadcasted_iota(
            jnp.int32, (count, LANES), 1
        )
        return jnp.sum(jnp.where(spot, flag, 0.0), axis=0, keepdims=True)

    tmpl_energy = tmpl_rows[rings] * on_lanes(circle, tail)
    for p in range(rings):
        tmpl_energy = tmpl_energy + tmpl_rows[p] * on_lanes(p * LANES, LANES)
    tmpl_energy = jnp.sum(tmpl_energy, axis=1, keepdims=True)
    box = None
    done = 0
    span = 1
    for bit in range(tmpl_len.bit_length()):
        if tmpl_len & span:
            moved = left(energy, done)
            box = moved if box is None else box + moved
            done += span
        if 2 * span <= tmpl_len:
            energy = energy + left(energy, span)
        span *= 2
    scores = crossed * lax.rsqrt(tmpl_energy * box[:, :lag_wide] + epsilon)
    scores_ref[...] = scores[:, :lag_count]

    pk[me] = jnp.max(scores, axis=0, keepdims=True)

    def swap(d):
        other = lax.rem(me + d, size)
        return pltpu.make_async_remote_copy(
            src_ref=pk.at[me],
            dst_ref=pk.at[me],
            send_sem=pk_send.at[d],
            recv_sem=pk_recv.at[d],
            device_id={"chan": other},
            device_id_type=MESH,
        )

    def swap_start(d, _):
        swap(d).start()
        return 0

    def swap_done(d, _):
        swap(d).wait_recv()
        return 0

    def swap_sent(d, _):
        swap(d).wait_send()
        return 0

    lax.fori_loop(1, size, swap_start, 0)
    lax.fori_loop(1, size, swap_done, 0)
    peaks_ref[...] = jnp.max(pk[...], axis=0)[:, :lag_count]
    lax.fori_loop(1, size, swap_sent, 0)
    for number, (when, src) in enumerate(sent):

        @pl.when(when)
        def _(number=number, src=src):
            pltpu.make_async_remote_copy(
                src_ref=src,
                dst_ref=src,
                send_sem=send_sem.at[number],
                recv_sem=recv_sem.at[0, 0],
                device_id={"chan": lax.rem(me + 1, size)},
                device_id_type=MESH,
            ).wait_send()


def hand_out(scores_in, peaks_in, scores_out, peaks_out, sems):
    copies = [
        pltpu.make_async_copy(scores_in, scores_out, sems.at[0]),
        pltpu.make_async_copy(peaks_in, peaks_out, sems.at[1]),
    ]
    for copy in copies:
        copy.start()
    for copy in copies:
        copy.wait()


def local(recording, alive, bank, start):
    ch_dev, length = recording.shape
    tmp_dev, tmpl_chans, tmpl_len = bank.shape
    lag_count = length - tmpl_len + 1
    size = lax.axis_size("chan")
    panels = -(-(length + 1) // LANES)
    rows = up(ch_dev + tmpl_chans - 1, SUB * 2)
    reach = -(-rows // ch_dev) - 1
    lag_wide = up(lag_count + SUB - 1, LANES)
    vmem = pl.BlockSpec(memory_space=pltpu.VMEM)
    anywhere = pl.BlockSpec(memory_space=pl.ANY)
    results = (
        jax.ShapeDtypeStruct((tmp_dev, lag_count), jnp.float32),
        jax.ShapeDtypeStruct((1, lag_count), jnp.float32),
    )
    scores, peaks = pl.pallas_call(
        functools.partial(kernel, size, tmpl_chans, tmpl_len, length, lag_count),
        out_shape=results,
        in_specs=[pl.BlockSpec(memory_space=pltpu.SMEM), vmem, anywhere, anywhere],
        out_specs=(vmem, vmem),
        scratch_shapes=[
            pltpu.VMEM((length, ch_dev), jnp.float32),
            pltpu.VMEM((LANES, ch_dev), jnp.float32),
            pltpu.VMEM((tmp_dev, tmpl_chans, tmpl_len), bank.dtype),
            pltpu.VMEM((tmp_dev, up(tmpl_len, 16), rows), bank.dtype),
            pltpu.VMEM((reach * ch_dev // LANES + 1, tmp_dev * SUB, LANES), jnp.float32),
            pltpu.VMEM((panels, rows, LANES), jnp.float32),
            pltpu.VMEM((panels, ch_dev, LANES), jnp.float32),
            pltpu.VMEM((panels, ch_dev, LANES), jnp.float32),
            pltpu.VMEM((rows, panels * LANES), jnp.bfloat16),
            pltpu.VMEM((lag_wide // LANES, tmp_dev * SUB, LANES), jnp.float32),
            pltpu.VMEM((panels, tmp_dev * SUB, LANES), jnp.float32),
            pltpu.VMEM((size, 1, lag_wide), jnp.float32),
            pltpu.SemaphoreType.DMA(()),
            pltpu.SemaphoreType.DMA((tmp_dev,)),
            pltpu.SemaphoreType.DMA((24,)),
            pltpu.SemaphoreType.DMA((reach, HALVES)),
            pltpu.SemaphoreType.DMA((HALVES,)),
            pltpu.SemaphoreType.DMA((size,)),
            pltpu.SemaphoreType.DMA((size,)),
        ],
        compiler_params=pltpu.CompilerParams(
            collective_id=0, has_side_effects=True, vmem_limit_bytes=60 * 1024 * 1024
        ),
    )(start, alive.reshape(1, ch_dev), recording.T, bank)
    scores, peaks = pl.pallas_call(
        hand_out,
        out_shape=results,
        in_specs=[anywhere, anywhere],
        out_specs=(anywhere, anywhere),
        scratch_shapes=[pltpu.SemaphoreType.DMA((2,))],
        compiler_params=pltpu.CompilerParams(vmem_limit_bytes=60 * 1024 * 1024),
    )(scores, peaks)
    return scores, peaks.reshape(lag_count)


def solution(mesh):
    placed = (
        P(("parts", "chan"), None),
        P(("parts", "chan")),
        P(("parts", "chan"), None, None),
        P(("parts", "chan")),
    )
    return jax.shard_map(
        local,
        mesh=mesh,
        in_specs=placed,
        out_specs=(P(("parts", "chan"), None), P("parts")),
        check_vma=False,
    )
```

```python
import functools

import jax
import jax.numpy as jnp
from jax import lax
from jax.experimental import pallas as pl
from jax.experimental.pallas import tpu as pltpu
from jax.sharding import PartitionSpec as P

epsilon = 1e-06
LANES = 128
SUB = 8
PIECES = 4
GROUP = 4
MESH = pl.DeviceIdType.MESH


def up(value, unit):
    return -(-value // unit) * unit


def left(x, by):
    by = by % x.shape[-1]
    return x if by == 0 else pltpu.roll(x, x.shape[-1] - by, x.ndim - 1)


def kernel(
    size, tmpl_chans, tmpl_len, length, lag_count,
    start_hbm, alive_hbm, rec_hbm, bank_hbm,
    scores_ref, peaks_ref,
    start_ref, alive_ref, rec_v, turn, bank_v, bank_t, tsq, xw, relay, x2, xb, esum, qsum, pk,
    rec_sem, start_sem, alive_sem, bank_sem, send_sem, recv_sem, relay_sem, pk_send, pk_recv,
):
    me = lax.axis_index("chan")
    ch_dev = rec_v.shape[1]
    tmp_dev = bank_v.shape[0]
    panels, rows, _ = xw.shape
    wide = panels * LANES
    lag_wide = up(lag_count + SUB - 1, LANES)
    reach = -(-rows // ch_dev) - 1
    tail_lane = length - (panels - 1) * LANES

    barrier = pltpu.get_barrier_semaphore()

    def greet(d, _):
        pl.semaphore_signal(
            barrier, inc=1, device_id={"chan": lax.rem(me + d, size)}, device_id_type=MESH
        )
        return 0

    lax.fori_loop(1, size, greet, 0)

    rec_copy = pltpu.make_async_copy(rec_hbm, rec_v, rec_sem)
    rec_copy.start()
    alive_copy = pltpu.make_async_copy(alive_hbm, alive_ref, alive_sem)
    alive_copy.start()
    start_copy = pltpu.make_async_copy(start_hbm, start_ref, start_sem)
    start_copy.start()
    bank_copies = [
        pltpu.make_async_copy(bank_hbm.at[k], bank_v.at[k], bank_sem.at[k])
        for k in range(tmp_dev)
    ]
    for copy in bank_copies:
        copy.start()

    alive_copy.wait()
    start_copy.wait()
    flags = alive_ref[...].astype(jnp.float32)
    turn[...] = jnp.zeros(turn.shape, jnp.float32)
    turn[tail_lane : tail_lane + 1, :] = flags
    rec_copy.wait()
    for p in range(panels - 1):
        xw[p, :ch_dev, :] = (rec_v[p * LANES : (p + 1) * LANES, :] * flags).T
    turn[:tail_lane, :] = rec_v[(panels - 1) * LANES : length, :] * flags
    xw[panels - 1, :ch_dev, :] = turn[...].T

    pl.semaphore_wait(barrier, size - 1)

    part = ch_dev // PIECES
    role = lax.rem(me, 4)
    further = me >= 4
    sent = []

    def rows_of(slot, h):
        return pl.ds(slot * ch_dev + h * part, part)

    def send(when, src, dst, arrival, by):
        copy = pltpu.make_async_remote_copy(
            src_ref=src,
            dst_ref=dst,
            send_sem=send_sem.at[len(sent)],
            recv_sem=arrival,
            device_id={"chan": lax.rem(me + by + size, size)},
            device_id_type=MESH,
        )
        sent.append((when, src))

        @pl.when(when)
        def _():
            copy.start()

    def to_slot(when, from_slot, h, slot, by):
        send(
            when,
            xw.at[:, rows_of(from_slot, h), :],
            xw.at[:, rows_of(slot, h), :],
            recv_sem.at[slot - 1, h],
            by,
        )

    def arrived(slot, h):
        where = xw.at[:, pl.ds(slot * ch_dev, tail) if slot == reach else rows_of(slot, h), :]
        pltpu.make_async_remote_copy(
            src_ref=where,
            dst_ref=where,
            send_sem=send_sem.at[0],
            recv_sem=recv_sem.at[slot - 1, h],
            device_id={"chan": lax.rem(me + 1, size)},
            device_id_type=MESH,
        ).wait_recv()

    is_a, is_b, is_c, is_d = (role == r for r in range(4))
    tail = rows - reach * ch_dev
    for h in range(PIECES):
        send(
            is_b & further,
            xw.at[:, rows_of(0, h), :],
            relay.at[:, pl.ds(h * part, part), :],
            relay_sem.at[h],
            2,
        )
        to_slot((is_a | is_c) & further, 0, h, 3, -3)
        to_slot(is_c | is_d, 0, h, 2, -2)
        to_slot(is_b | is_d, 0, h, 1, -1)
    send(
        further,
        xw.at[:, pl.ds(0, tail), :],
        xw.at[:, pl.ds(reach * ch_dev, tail), :],
        recv_sem.at[reach - 1, 0],
        -4,
    )
    for d in range(1, reach + 1):
        count = min(ch_dev, rows - d * ch_dev)

        @pl.when(me + d >= size)
        def _(d=d, count=count):
            xw[:, d * ch_dev : d * ch_dev + count, :] = jnp.zeros(
                (panels, count, LANES), jnp.float32
            )

    def pass_on(when, from_slot, h, slot, by):
        @pl.when(when)
        def _():
            arrived(from_slot, h)

        to_slot(when, from_slot, h, slot, by)

    def pass_back(h):
        when = back

        @pl.when(when)
        def _():
            where = relay.at[:, pl.ds(h * part, part), :]
            pltpu.make_async_remote_copy(
                src_ref=where,
                dst_ref=where,
                send_sem=send_sem.at[0],
                recv_sem=relay_sem.at[h],
                device_id={"chan": lax.rem(me + 1, size)},
                device_id_type=MESH,
            ).wait_recv()

        send(
            when,
            relay.at[:, pl.ds(h * part, part), :],
            xw.at[:, rows_of(2, h), :],
            recv_sem.at[1, h],
            -4,
        )

    back = is_d & further
    b_in, d_in = is_b & (me + 3 < size), is_d & (me + 1 < size)

    def relay_round(number):
        if number < PIECES:
            pass_on(b_in, 3, number, 1, 2)
            pass_back(number)
        if number % 2:
            pass_on(is_a, 2, number // 2, 1, 1)
            pass_on(is_b, 2, number // 2, 3, -1)
        if number >= PIECES:
            pass_on(d_in, 1, number - PIECES, 2, -1)
            pass_on(d_in, 2, number - PIECES, 3, -1)

    circle = reach * ch_dev
    rings = circle // LANES
    lane_t = lax.broadcasted_iota(jnp.int32, (tmpl_len, LANES), 1)
    row_id = lax.broadcasted_iota(jnp.int32, (ch_dev, LANES), 0)
    for p in range(panels):
        x2[p] = jnp.square(xw[p, :ch_dev, :])

    eye = (
        lax.broadcasted_iota(jnp.int32, (tmpl_len, tmpl_len), 0)
        == lax.broadcasted_iota(jnp.int32, (tmpl_len, tmpl_len), 1)
    ).astype(bank_v.dtype)

    def offset_of(k):
        return jnp.clip(start_ref[k] - me * ch_dev, 0, ch_dev - 1)

    def fold(x):
        return jnp.sum(x.reshape(x.shape[0] // SUB, SUB, x.shape[1]), axis=0)

    def block_of(k):
        return pl.ds(pl.multiple_of(k * SUB, SUB), SUB)

    def prepare(k, _):
        pltpu.make_async_copy(bank_hbm.at[k], bank_v.at[k], bank_sem.at[k]).wait()
        offset = offset_of(k)
        wide_t = jnp.concatenate(
            [
                lax.dot_general(
                    eye,
                    bank_v[k],
                    (((1,), (1,)), ((), ())),
                    preferred_element_type=jnp.float32,
                ),
                jnp.zeros((tmpl_len, circle - tmpl_chans), jnp.float32),
            ],
            axis=1,
        )
        turned = [
            pltpu.roll(wide_t[:, p * LANES : (p + 1) * LANES], offset, 1) for p in range(rings)
        ]
        wraps = lane_t < offset
        for p in range(rings + 1):
            piece = jnp.where(
                wraps, turned[p - 1] if p else 0.0, turned[p] if p < rings else 0.0
            )
            tsq[p, block_of(k), :] = fold(piece * piece)
            lanes = min(LANES, rows - p * LANES)
            bank_t[k, :tmpl_len, p * LANES : p * LANES + lanes] = piece[:, :lanes].astype(
                bank_t.dtype
            )
        inside = row_id >= offset
        for p in range(panels):
            qsum[p, block_of(k), :] = fold(jnp.where(inside, x2[p], 0.0))
        return 0

    each = tmp_dev // (2 * PIECES)

    def prepare_some(j, _):
        for u in range(each):
            prepare(each * j + u, 0)
        for number in range(2 * PIECES):

            @pl.when(j == number)
            def _(number=number):
                relay_round(number)

        return 0

    lax.fori_loop(0, 2 * PIECES, prepare_some, 0)

    for d in range(1, reach + 1):
        for h in range(PIECES if d < reach else 1):
            waited = {1: d_in, 2: is_a | is_b | d_in, 3: b_in}.get(d)
            here = me + d < size
            if waited is not None:
                here = here & jnp.logical_not(waited)

            @pl.when(here)
            def _(d=d, h=h):
                arrived(d, h)

    for p in range(panels):
        xb[:, p * LANES : (p + 1) * LANES] = xw[p].astype(jnp.bfloat16)
    common = [fold(jnp.square(xw[p, ch_dev:tmpl_chans, :])) for p in range(panels)]
    for p in range(panels):
        x2[p] = jnp.square(xw[p, tmpl_chans : tmpl_chans + ch_dev, :])
    skip = ((panels - 1) * LANES - lag_count + 1) // 16 * 16

    main = panels - 1
    tall = bank_t.shape[1]

    def sum_diagonals(k, acc, last):
        half = LANES
        high = jnp.concatenate([acc[half:, half:], last[half - skip :]], axis=1)
        acc = jnp.concatenate([acc[: tmpl_len - half] + high, acc[tmpl_len - half : half]], axis=0)
        edge = last[: half - skip]
        half //= 2
        edge = jnp.concatenate(
            [jnp.zeros((half - edge.shape[0], LANES), jnp.float32), edge], axis=0
        )
        high = left(jnp.concatenate([acc[half:], edge], axis=1), half)
        acc = acc[:half] + high[:, : main * LANES]
        while half > SUB:
            half //= 2
            acc = acc[:half] + left(acc[half:], half)
        for p in range(main):
            esum[p, block_of(k), :] = acc[:, p * LANES : (p + 1) * LANES]

    def correlate(g, _):
        group = pl.ds(g * GROUP, GROUP)
        accs = jnp.dot(
            bank_t[group].reshape(GROUP * tall, rows),
            xb[:, : main * LANES],
            preferred_element_type=jnp.float32,
        )
        lasts = jnp.dot(
            bank_t[group, skip:, :].reshape(GROUP * (tall - skip), rows),
            xb[:, main * LANES :],
            preferred_element_type=jnp.float32,
        )
        for u in range(GROUP):
            k = g * GROUP + u
            inside = row_id < offset_of(k)
            for p in range(panels):
                qsum[p, block_of(k), :] += common[p] + fold(jnp.where(inside, x2[p], 0.0))
            start = u * (tall - skip)
            sum_diagonals(
                k,
                accs[u * tall : u * tall + tmpl_len],
                lasts[start : start + tmpl_len - skip],
            )
        return 0

    lax.fori_loop(0, tmp_dev // GROUP, correlate, 0)

    crossed = jnp.zeros((tmp_dev, lag_wide), jnp.float32)
    energy = jnp.zeros((tmp_dev, wide), jnp.float32)
    tmpl_rows = [jnp.zeros((tmp_dev, LANES), jnp.float32) for _ in range(rings + 1)]
    for b in range(SUB):
        pick = pl.ds(b, tmp_dev, stride=SUB)
        crossed = crossed + left(
            jnp.concatenate([esum[p, pick, :] for p in range(lag_wide // LANES)], axis=1), b
        )
        energy = energy + jnp.concatenate([qsum[p, pick, :] for p in range(panels)], axis=1)
        tmpl_rows = [tmpl_rows[p] + tsq[p, pick, :] for p in range(rings + 1)]
    def on_lanes(first, count):
        flag = xw[panels - 1, first : first + count, tail_lane : tail_lane + 1]
        spot = lax.broadcasted_iota(jnp.int32, (count, LANES), 0) == lax.broadcasted_iota(
            jnp.int32, (count, LANES), 1
        )
        return jnp.sum(jnp.where(spot, flag, 0.0), axis=0, keepdims=True)

    tmpl_energy = tmpl_rows[rings] * on_lanes(circle, tail)
    for p in range(rings):
        tmpl_energy = tmpl_energy + tmpl_rows[p] * on_lanes(p * LANES, LANES)
    tmpl_energy = jnp.sum(tmpl_energy, axis=1, keepdims=True)
    box = None
    done = 0
    span = 1
    for bit in range(tmpl_len.bit_length()):
        if tmpl_len & span:
            moved = left(energy, done)
            box = moved if box is None else box + moved
            done += span
        if 2 * span <= tmpl_len:
            energy = energy + left(energy, span)
        span *= 2
    scores = crossed * lax.rsqrt(tmpl_energy * box[:, :lag_wide] + epsilon)
    scores_ref[...] = scores[:, :lag_count]

    pk[me] = jnp.max(scores, axis=0, keepdims=True)

    def swap(d):
        other = lax.rem(me + d, size)
        return pltpu.make_async_remote_copy(
            src_ref=pk.at[me],
            dst_ref=pk.at[me],
            send_sem=pk_send.at[d],
            recv_sem=pk_recv.at[d],
            device_id={"chan": other},
            device_id_type=MESH,
        )

    def swap_start(d, _):
        swap(d).start()
        return 0

    def swap_done(d, _):
        swap(d).wait_recv()
        return 0

    def swap_sent(d, _):
        swap(d).wait_send()
        return 0

    lax.fori_loop(1, size, swap_start, 0)
    lax.fori_loop(1, size, swap_done, 0)
    peaks_ref[...] = jnp.max(pk[...], axis=0)[:, :lag_count]
    lax.fori_loop(1, size, swap_sent, 0)
    for number, (when, src) in enumerate(sent):

        @pl.when(when)
        def _(number=number, src=src):
            pltpu.make_async_remote_copy(
                src_ref=src,
                dst_ref=src,
                send_sem=send_sem.at[number],
                recv_sem=recv_sem.at[0, 0],
                device_id={"chan": lax.rem(me + 1, size)},
                device_id_type=MESH,
            ).wait_send()


def hand_out(scores_in, peaks_in, scores_out, peaks_out, sems):
    copies = [
        pltpu.make_async_copy(scores_in, scores_out, sems.at[0]),
        pltpu.make_async_copy(peaks_in, peaks_out, sems.at[1]),
    ]
    for copy in copies:
        copy.start()
    for copy in copies:
        copy.wait()


def local(recording, alive, bank, start):
    ch_dev, length = recording.shape
    tmp_dev, tmpl_chans, tmpl_len = bank.shape
    lag_count = length - tmpl_len + 1
    size = lax.axis_size("chan")
    panels = -(-(length + 1) // LANES)
    rows = up(ch_dev + tmpl_chans - 1, SUB * 2)
    reach = -(-rows // ch_dev) - 1
    lag_wide = up(lag_count + SUB - 1, LANES)
    vmem = pl.BlockSpec(memory_space=pltpu.VMEM)
    far = pl.BlockSpec(memory_space=pltpu.HBM)
    results = (
        jax.ShapeDtypeStruct((tmp_dev, lag_count), jnp.float32),
        jax.ShapeDtypeStruct((1, lag_count), jnp.float32),
    )
    scores, peaks = pl.pallas_call(
        functools.partial(kernel, size, tmpl_chans, tmpl_len, length, lag_count),
        out_shape=results,
        in_specs=[far] * 4,
        out_specs=(vmem, vmem),
        scratch_shapes=[
            pltpu.SMEM((tmp_dev,), jnp.int32),
            pltpu.VMEM((1, ch_dev), jnp.int32),
            pltpu.VMEM((length, ch_dev), jnp.float32),
            pltpu.VMEM((LANES, ch_dev), jnp.float32),
            pltpu.VMEM((tmp_dev, tmpl_chans, tmpl_len), bank.dtype),
            pltpu.VMEM((tmp_dev, up(tmpl_len, 16), rows), bank.dtype),
            pltpu.VMEM((reach * ch_dev // LANES + 1, tmp_dev * SUB, LANES), jnp.float32),
            pltpu.VMEM((panels, rows, LANES), jnp.float32),
            pltpu.VMEM((panels, ch_dev, LANES), jnp.float32),
            pltpu.VMEM((panels, ch_dev, LANES), jnp.float32),
            pltpu.VMEM((rows, panels * LANES), jnp.bfloat16),
            pltpu.VMEM((lag_wide // LANES, tmp_dev * SUB, LANES), jnp.float32),
            pltpu.VMEM((panels, tmp_dev * SUB, LANES), jnp.float32),
            pltpu.VMEM((size, 1, lag_wide), jnp.float32),
            pltpu.SemaphoreType.DMA(()),
            pltpu.SemaphoreType.DMA(()),
            pltpu.SemaphoreType.DMA(()),
            pltpu.SemaphoreType.DMA((tmp_dev,)),
            pltpu.SemaphoreType.DMA((12 * PIECES,)),
            pltpu.SemaphoreType.DMA((reach, PIECES)),
            pltpu.SemaphoreType.DMA((PIECES,)),
            pltpu.SemaphoreType.DMA((size,)),
            pltpu.SemaphoreType.DMA((size,)),
        ],
        compiler_params=pltpu.CompilerParams(
            collective_id=0, has_side_effects=True, vmem_limit_bytes=60 * 1024 * 1024
        ),
    )(start, alive.reshape(1, ch_dev), recording.T, bank)
    scores, peaks = pl.pallas_call(
        hand_out,
        out_shape=results,
        in_specs=[far] * 2,
        out_specs=(far, far),
        scratch_shapes=[pltpu.SemaphoreType.DMA((2,))],
        compiler_params=pltpu.CompilerParams(vmem_limit_bytes=60 * 1024 * 1024),
    )(scores, peaks)
    return scores, peaks.reshape(lag_count)


def solution(mesh):
    placed = (
        P(("parts", "chan"), None),
        P(("parts", "chan")),
        P(("parts", "chan"), None, None),
        P(("parts", "chan")),
    )
    return jax.shard_map(
        local,
        mesh=mesh,
        in_specs=placed,
        out_specs=(P(("parts", "chan"), None), P("parts")),
        check_vma=False,
    )
```

```python
import functools

import jax
import jax.numpy as jnp
from jax import lax
from jax.experimental import pallas as pl
from jax.experimental.pallas import tpu as pltpu
from jax.sharding import PartitionSpec as P

epsilon = 1e-06
LANES = 128
SUB = 8
PIECES = 4
MESH = pl.DeviceIdType.MESH


def up(value, unit):
    return -(-value // unit) * unit


def left(x, by):
    by = by % x.shape[-1]
    return x if by == 0 else pltpu.roll(x, x.shape[-1] - by, x.ndim - 1)


def kernel(
    size, tmpl_chans, tmpl_len, length, lag_count,
    start_hbm, alive_hbm, rec_hbm, bank_hbm,
    scores_ref, peaks_ref,
    start_ref, alive_ref, rec_v, turn, bank_v, bank_t, tsq, xw, relay, x2, xb, offv, esum, qsum, pk,
    rec_sem, start_sem, alive_sem, bank_sem, send_sem, recv_sem, relay_sem, pk_send, pk_recv,
):
    me = lax.axis_index("chan")
    ch_dev = rec_v.shape[1]
    tmp_dev = bank_v.shape[0]
    panels, rows, _ = xw.shape
    wide = panels * LANES
    lag_wide = up(lag_count + SUB - 1, LANES)
    reach = -(-rows // ch_dev) - 1
    tail_lane = length - (panels - 1) * LANES

    barrier = pltpu.get_barrier_semaphore()

    def greet(d, _):
        pl.semaphore_signal(
            barrier, inc=1, device_id={"chan": lax.rem(me + d, size)}, device_id_type=MESH
        )
        return 0

    lax.fori_loop(1, size, greet, 0)

    rec_copy = pltpu.make_async_copy(rec_hbm, rec_v, rec_sem)
    rec_copy.start()
    alive_copy = pltpu.make_async_copy(alive_hbm, alive_ref, alive_sem)
    alive_copy.start()
    start_copy = pltpu.make_async_copy(start_hbm, start_ref, start_sem)
    start_copy.start()
    bank_copies = [
        pltpu.make_async_copy(bank_hbm.at[k], bank_v.at[k], bank_sem.at[k])
        for k in range(tmp_dev)
    ]
    for copy in bank_copies:
        copy.start()

    alive_copy.wait()
    start_copy.wait()
    flags = alive_ref[...].astype(jnp.float32)
    turn[...] = jnp.zeros(turn.shape, jnp.float32)
    turn[tail_lane : tail_lane + 1, :] = flags
    rec_copy.wait()
    for p in range(panels - 1):
        xw[p, :ch_dev, :] = (rec_v[p * LANES : (p + 1) * LANES, :] * flags).T
    turn[:tail_lane, :] = rec_v[(panels - 1) * LANES : length, :] * flags
    xw[panels - 1, :ch_dev, :] = turn[...].T

    pl.semaphore_wait(barrier, size - 1)

    part = ch_dev // PIECES
    role = lax.rem(me, 4)
    further = me >= 4
    sent = []

    def rows_of(slot, h):
        return pl.ds(slot * ch_dev + h * part, part)

    def send(when, src, dst, arrival, by):
        copy = pltpu.make_async_remote_copy(
            src_ref=src,
            dst_ref=dst,
            send_sem=send_sem.at[len(sent)],
            recv_sem=arrival,
            device_id={"chan": lax.rem(me + by + size, size)},
            device_id_type=MESH,
        )
        sent.append((when, src))

        @pl.when(when)
        def _():
            copy.start()

    def to_slot(when, from_slot, h, slot, by):
        send(
            when,
            xw.at[:, rows_of(from_slot, h), :],
            xw.at[:, rows_of(slot, h), :],
            recv_sem.at[slot - 1, h],
            by,
        )

    def arrived(slot, h):
        where = xw.at[:, pl.ds(slot * ch_dev, tail) if slot == reach else rows_of(slot, h), :]
        pltpu.make_async_remote_copy(
            src_ref=where,
            dst_ref=where,
            send_sem=send_sem.at[0],
            recv_sem=recv_sem.at[slot - 1, h],
            device_id={"chan": lax.rem(me + 1, size)},
            device_id_type=MESH,
        ).wait_recv()

    is_a, is_b, is_c, is_d = (role == r for r in range(4))
    tail = rows - reach * ch_dev
    for h in range(PIECES):
        send(
            is_b & further,
            xw.at[:, rows_of(0, h), :],
            relay.at[:, pl.ds(h * part, part), :],
            relay_sem.at[h],
            2,
        )
        to_slot((is_a | is_c) & further, 0, h, 3, -3)
        to_slot(is_c | is_d, 0, h, 2, -2)
        to_slot(is_b | is_d, 0, h, 1, -1)
    send(
        further,
        xw.at[:, pl.ds(0, tail), :],
        xw.at[:, pl.ds(reach * ch_dev, tail), :],
        recv_sem.at[reach - 1, 0],
        -4,
    )
    for d in range(1, reach + 1):
        count = min(ch_dev, rows - d * ch_dev)

        @pl.when(me + d >= size)
        def _(d=d, count=count):
            xw[:, d * ch_dev : d * ch_dev + count, :] = jnp.zeros(
                (panels, count, LANES), jnp.float32
            )

    def pass_on(when, from_slot, h, slot, by):
        @pl.when(when)
        def _():
            arrived(from_slot, h)

        to_slot(when, from_slot, h, slot, by)

    def pass_back(h):
        when = back

        @pl.when(when)
        def _():
            where = relay.at[:, pl.ds(h * part, part), :]
            pltpu.make_async_remote_copy(
                src_ref=where,
                dst_ref=where,
                send_sem=send_sem.at[0],
                recv_sem=relay_sem.at[h],
                device_id={"chan": lax.rem(me + 1, size)},
                device_id_type=MESH,
            ).wait_recv()

        send(
            when,
            relay.at[:, pl.ds(h * part, part), :],
            xw.at[:, rows_of(2, h), :],
            recv_sem.at[1, h],
            -4,
        )

    back = is_d & further
    b_in, d_in = is_b & (me + 3 < size), is_d & (me + 1 < size)

    def relay_round(number):
        if number < PIECES:
            pass_on(b_in, 3, number, 1, 2)
            pass_back(number)
        if number % 2:
            pass_on(is_a, 2, number // 2, 1, 1)
            pass_on(is_b, 2, number // 2, 3, -1)
        if number >= PIECES:
            pass_on(d_in, 1, number - PIECES, 2, -1)
            pass_on(d_in, 2, number - PIECES, 3, -1)

    circle = reach * ch_dev
    rings = circle // LANES
    lane_t = lax.broadcasted_iota(jnp.int32, (tmpl_len, LANES), 1)
    row_id = lax.broadcasted_iota(jnp.int32, (ch_dev, LANES), 0)
    for p in range(panels):
        x2[p] = jnp.square(xw[p, :ch_dev, :])

    eye = (
        lax.broadcasted_iota(jnp.int32, (tmpl_len, tmpl_len), 0)
        == lax.broadcasted_iota(jnp.int32, (tmpl_len, tmpl_len), 1)
    ).astype(bank_v.dtype)

    def offset_of(k):
        return jnp.clip(start_ref[k] - me * ch_dev, 0, ch_dev - 1)

    def fold(x):
        return jnp.sum(x.reshape(x.shape[0] // SUB, SUB, x.shape[1]), axis=0)

    def block_of(k):
        return pl.ds(pl.multiple_of(k * SUB, SUB), SUB)

    def prepare(k, _):
        pltpu.make_async_copy(bank_hbm.at[k], bank_v.at[k], bank_sem.at[k]).wait()
        offset = offset_of(k)
        wide_t = jnp.concatenate(
            [
                lax.dot_general(
                    eye,
                    bank_v[k],
                    (((1,), (1,)), ((), ())),
                    preferred_element_type=jnp.float32,
                ),
                jnp.zeros((tmpl_len, circle - tmpl_chans), jnp.float32),
            ],
            axis=1,
        )
        turned = [
            pltpu.roll(wide_t[:, p * LANES : (p + 1) * LANES], offset, 1) for p in range(rings)
        ]
        wraps = lane_t < offset
        for p in range(rings):
            piece = jnp.where(wraps, turned[p - 1], turned[p])
            bank_t[k, :, p * LANES : (p + 1) * LANES] = piece.astype(bank_t.dtype)
            tsq[p, block_of(k), :] = fold(piece * piece)
        offv[block_of(k), :] = jnp.full((SUB, LANES), offset, jnp.int32)
        inside = row_id >= offset
        for p in range(panels):
            qsum[p, block_of(k), :] = fold(jnp.where(inside, x2[p], 0.0))
        return 0

    each = tmp_dev // (2 * PIECES)

    def prepare_some(j, _):
        for u in range(each):
            prepare(each * j + u, 0)
        for number in range(2 * PIECES):

            @pl.when(j == number)
            def _(number=number):
                relay_round(number)

        return 0

    lax.fori_loop(0, 2 * PIECES, prepare_some, 0)

    for d in range(1, reach + 1):
        for h in range(PIECES if d < reach else 1):
            waited = {1: d_in, 2: is_a | is_b | d_in, 3: b_in}.get(d)
            here = me + d < size
            if waited is not None:
                here = here & jnp.logical_not(waited)

            @pl.when(here)
            def _(d=d, h=h):
                arrived(d, h)

    for p in range(panels):
        columns = slice(p * LANES, (p + 1) * LANES)
        rounded = xw[p, :circle, :].astype(jnp.bfloat16)
        xb[0, :, columns] = rounded
        xb[1, tail:, columns] = rounded[tail:]
        xb[1, :tail, columns] = xw[p, circle:, :].astype(jnp.bfloat16)
    common = [fold(jnp.square(xw[p, ch_dev:tmpl_chans, :])) for p in range(panels)]
    for p in range(panels):
        x2[p] = jnp.square(xw[p, tmpl_chans : tmpl_chans + ch_dev, :])
    skip = ((panels - 1) * LANES - lag_count + 1) // 16 * 16

    def correlate(k, _):
        offset = offset_of(k)
        inside = row_id < offset
        for p in range(panels):
            qsum[p, block_of(k), :] += common[p] + fold(jnp.where(inside, x2[p], 0.0))
        data = xb.at[(offset + tmpl_chans > circle).astype(jnp.int32)]
        main = panels - 1
        acc = jnp.dot(
            bank_t[k], data[:, : main * LANES], preferred_element_type=jnp.float32
        )
        last = jnp.dot(
            bank_t[k, skip:, :], data[:, main * LANES :], preferred_element_type=jnp.float32
        )
        half = LANES
        high = jnp.concatenate([acc[half:, half:], last[half - skip :]], axis=1)
        acc = jnp.concatenate([acc[: tmpl_len - half] + high, acc[tmpl_len - half : half]], axis=0)
        edge = last[: half - skip]
        half //= 2
        edge = jnp.concatenate(
            [jnp.zeros((half - edge.shape[0], LANES), jnp.float32), edge], axis=0
        )
        high = left(jnp.concatenate([acc[half:], edge], axis=1), half)
        acc = acc[:half] + high[:, : main * LANES]
        while half > SUB:
            half //= 2
            acc = acc[:half] + left(acc[half:], half)
        for p in range(main):
            esum[p, block_of(k), :] = acc[:, p * LANES : (p + 1) * LANES]
        return 0

    lax.fori_loop(0, tmp_dev, correlate, 0, unroll=4)

    crossed = jnp.zeros((tmp_dev, lag_wide), jnp.float32)
    energy = jnp.zeros((tmp_dev, wide), jnp.float32)
    tmpl_rows = [jnp.zeros((tmp_dev, LANES), jnp.float32) for _ in range(rings)]
    for b in range(SUB):
        pick = pl.ds(b, tmp_dev, stride=SUB)
        crossed = crossed + left(
            jnp.concatenate([esum[p, pick, :] for p in range(lag_wide // LANES)], axis=1), b
        )
        energy = energy + jnp.concatenate([qsum[p, pick, :] for p in range(panels)], axis=1)
        tmpl_rows = [tmpl_rows[p] + tsq[p, pick, :] for p in range(rings)]
    def on_lanes(first, count):
        flag = xw[panels - 1, first : first + count, tail_lane : tail_lane + 1]
        spot = lax.broadcasted_iota(jnp.int32, (count, LANES), 0) == lax.broadcasted_iota(
            jnp.int32, (count, LANES), 1
        )
        return jnp.sum(jnp.where(spot, flag, 0.0), axis=0, keepdims=True)

    live = [on_lanes(p * LANES, LANES) for p in range(rings)]
    lane_k = lax.broadcasted_iota(jnp.int32, (tmp_dev, LANES), 1)
    wrapped = (offv[pl.ds(0, tmp_dev, stride=SUB), :] + tmpl_chans > circle) & (lane_k < tail)
    tmpl_energy = tmpl_rows[0] * jnp.where(wrapped, on_lanes(circle, tail), live[0])
    for p in range(1, rings):
        tmpl_energy = tmpl_energy + tmpl_rows[p] * live[p]
    tmpl_energy = jnp.sum(tmpl_energy, axis=1, keepdims=True)
    box = None
    done = 0
    span = 1
    for bit in range(tmpl_len.bit_length()):
        if tmpl_len & span:
            moved = left(energy, done)
            box = moved if box is None else box + moved
            done += span
        if 2 * span <= tmpl_len:
            energy = energy + left(energy, span)
        span *= 2
    scores = crossed * lax.rsqrt(tmpl_energy * box[:, :lag_wide] + epsilon)
    scores_ref[...] = scores[:, :lag_count]

    pk[me] = jnp.max(scores, axis=0, keepdims=True)

    def swap(d):
        other = lax.rem(me + d, size)
        return pltpu.make_async_remote_copy(
            src_ref=pk.at[me],
            dst_ref=pk.at[me],
            send_sem=pk_send.at[d],
            recv_sem=pk_recv.at[d],
            device_id={"chan": other},
            device_id_type=MESH,
        )

    def swap_start(d, _):
        swap(d).start()
        return 0

    def swap_done(d, _):
        swap(d).wait_recv()
        return 0

    def swap_sent(d, _):
        swap(d).wait_send()
        return 0

    lax.fori_loop(1, size, swap_start, 0)
    lax.fori_loop(1, size, swap_done, 0)
    peaks_ref[...] = jnp.max(pk[...], axis=0)[:, :lag_count]
    lax.fori_loop(1, size, swap_sent, 0)
    for number, (when, src) in enumerate(sent):

        @pl.when(when)
        def _(number=number, src=src):
            pltpu.make_async_remote_copy(
                src_ref=src,
                dst_ref=src,
                send_sem=send_sem.at[number],
                recv_sem=recv_sem.at[0, 0],
                device_id={"chan": lax.rem(me + 1, size)},
                device_id_type=MESH,
            ).wait_send()


def hand_out(scores_in, peaks_in, scores_out, peaks_out, sems):
    copies = [
        pltpu.make_async_copy(scores_in, scores_out, sems.at[0]),
        pltpu.make_async_copy(peaks_in, peaks_out, sems.at[1]),
    ]
    for copy in copies:
        copy.start()
    for copy in copies:
        copy.wait()


def local(recording, alive, bank, start):
    ch_dev, length = recording.shape
    tmp_dev, tmpl_chans, tmpl_len = bank.shape
    lag_count = length - tmpl_len + 1
    size = lax.axis_size("chan")
    panels = -(-(length + 1) // LANES)
    rows = up(ch_dev + tmpl_chans - 1, SUB * 2)
    reach = -(-rows // ch_dev) - 1
    lag_wide = up(lag_count + SUB - 1, LANES)
    vmem = pl.BlockSpec(memory_space=pltpu.VMEM)
    anywhere = pl.BlockSpec(memory_space=pl.ANY)
    results = (
        jax.ShapeDtypeStruct((tmp_dev, lag_count), jnp.float32),
        jax.ShapeDtypeStruct((1, lag_count), jnp.float32),
    )
    scores, peaks = pl.pallas_call(
        functools.partial(kernel, size, tmpl_chans, tmpl_len, length, lag_count),
        out_shape=results,
        in_specs=[anywhere] * 4,
        out_specs=(vmem, vmem),
        scratch_shapes=[
            pltpu.SMEM((tmp_dev,), jnp.int32),
            pltpu.VMEM((1, ch_dev), jnp.int32),
            pltpu.VMEM((length, ch_dev), jnp.float32),
            pltpu.VMEM((LANES, ch_dev), jnp.float32),
            pltpu.VMEM((tmp_dev, tmpl_chans, tmpl_len), bank.dtype),
            pltpu.VMEM((tmp_dev, tmpl_len, reach * ch_dev), bank.dtype),
            pltpu.VMEM((reach * ch_dev // LANES, tmp_dev * SUB, LANES), jnp.float32),
            pltpu.VMEM((panels, rows, LANES), jnp.float32),
            pltpu.VMEM((panels, ch_dev, LANES), jnp.float32),
            pltpu.VMEM((panels, ch_dev, LANES), jnp.float32),
            pltpu.VMEM((2, reach * ch_dev, panels * LANES), jnp.bfloat16),
            pltpu.VMEM((tmp_dev * SUB, LANES), jnp.int32),
            pltpu.VMEM((lag_wide // LANES, tmp_dev * SUB, LANES), jnp.float32),
            pltpu.VMEM((panels, tmp_dev * SUB, LANES), jnp.float32),
            pltpu.VMEM((size, 1, lag_wide), jnp.float32),
            pltpu.SemaphoreType.DMA(()),
            pltpu.SemaphoreType.DMA(()),
            pltpu.SemaphoreType.DMA(()),
            pltpu.SemaphoreType.DMA((tmp_dev,)),
            pltpu.SemaphoreType.DMA((12 * PIECES,)),
            pltpu.SemaphoreType.DMA((reach, PIECES)),
            pltpu.SemaphoreType.DMA((PIECES,)),
            pltpu.SemaphoreType.DMA((size,)),
            pltpu.SemaphoreType.DMA((size,)),
        ],
        compiler_params=pltpu.CompilerParams(
            collective_id=0, has_side_effects=True, vmem_limit_bytes=60 * 1024 * 1024
        ),
    )(start, alive.reshape(1, ch_dev), recording.T, bank)
    scores, peaks = pl.pallas_call(
        hand_out,
        out_shape=results,
        in_specs=[anywhere, anywhere],
        out_specs=(anywhere, anywhere),
        scratch_shapes=[pltpu.SemaphoreType.DMA((2,))],
        compiler_params=pltpu.CompilerParams(vmem_limit_bytes=60 * 1024 * 1024),
    )(scores, peaks)
    return scores, peaks.reshape(lag_count)


def solution(mesh):
    placed = (
        P(("parts", "chan"), None),
        P(("parts", "chan")),
        P(("parts", "chan"), None, None),
        P(("parts", "chan")),
    )
    return jax.shard_map(
        local,
        mesh=mesh,
        in_specs=placed,
        out_specs=(P(("parts", "chan"), None), P("parts")),
        check_vma=False,
    )
```
